256 devices in a mesh: dp: 16 (over x, z_lo), tensor: 16 (over y, z_hi, core).
Axes of the slice: x: 4, y: 4, z: 8 (z_hi: 2, z_lo: 4; z = z_hi * 4 + z_lo), core: 2. Of those that a mesh axis runs over, the one named last changes fastest.
Arguments:
- tokens: bfloat16 [6144, 2048], P('dp', 'tensor'), may hold values from -6 to 6
- cotangent: bfloat16 [6144, 2048], P('dp', 'tensor'), may hold values from -6 to 6
- prefix: int32 [48], P('dp'), may hold values from 2048 to 16384, as said below
- gate_weight: bfloat16 [2048, 16384], P('dp', 'tensor'), may hold values from -0.125 to 0.125
- up_weight: bfloat16 [2048, 16384], P('dp', 'tensor'), may hold values from -0.125 to 0.125
- down_weight: bfloat16 [16384, 2048], P('tensor', 'dp'), may hold values from -0.046875 to 0.046875
Outputs:
- mixed: bfloat16 [6144, 2048], P('dp', 'tensor')
- input_grad: bfloat16 [6144, 2048], P('dp', 'tensor')
- gate_grad: bfloat16 [2048, 16384], P('dp', 'tensor')
- up_grad: bfloat16 [2048, 16384], P('dp', 'tensor')
- down_grad: bfloat16 [16384, 2048], P('tensor', 'dp')
The draws below stay inside these ranges and needn't reach their ends.
Inputs may be any that keep to these rules, and one draw needn't show every extreme that they name: `prefix`: every entry is 2048, 4096, 8192 or 16384.
All inputs are finite; a program needn't handle non-finite values.
Results may differ from the reference program's by a relative error of at most 0.02.
Values may be sent and summed in bfloat16 or wider, within the bound.
No kernel may reach another device: no remote copies, remote signals or barrier semaphores. Data moves between devices by JAX's collectives and lax.ppermute only.
A program may use at most 128 MiB of HBM per device.

```python
import math
import jax
import jax.numpy as jnp
from jax import lax

D = 2048
FF = 16384
GROUP = 128
TOK_DEV = 384
TOKENS = 6144
N_DP = 16


def draw_prefix(key, part):
    key = jax.random.fold_in(key, 7)
    key_level, key_full, key_least = jax.random.split(key, 3)
    group_count = TOKENS // GROUP
    levels = jax.random.randint(key_level, (group_count,), 0, 4)
    full_slot = jax.random.randint(key_full, (), 0, group_count)
    least_slot = (full_slot + 1 + jax.random.randint(key_least, (), 0, group_count - 1)) % group_count
    levels = levels.at[full_slot].set(3).at[least_slot].set(0)
    return (FF // 8 * jnp.left_shift(jnp.int32(1), levels)).astype(jnp.int32)


def with_spikes(array, own_key, source, target, parts, factor):
    def block_of(dim):
        return (jnp.arange(array.shape[dim]) // (array.shape[dim] // parts)).reshape((-1,) + (1,) * (array.ndim - 1 - dim))

    first = jax.random.permutation(own_key, parts)[block_of(target)]
    second = (block_of(target) + parts // 2) % parts
    return jnp.where((block_of(source) == first) | (block_of(source) == second), factor * array, array)


def level_of(stream_key, dims, cuts, low, top_value):
    def one(position, shards_of):
        heights = jax.random.uniform(jax.random.fold_in(jax.random.fold_in(stream_key, 6), position), (shards_of,), jnp.float32, low / len(cuts), top_value / len(cuts))
        return jnp.repeat(jnp.exp(heights), dims[position] // shards_of).reshape((-1,) + (1,) * (len(dims) - position - 1))

    factor_of = one(*cuts[0])
    for cut in cuts[1:]:
        factor_of = factor_of * one(*cut)
    return factor_of


def scatter_about(stream_key, extent, spread, limit, cuts=(), held_as=jnp.bfloat16):
    loudness = level_of(stream_key, extent, cuts, -0.22, 0.18) if cuts else 1.0
    values = jax.random.normal(stream_key, extent, jnp.float32) * spread * loudness
    return jnp.minimum(jnp.maximum(values, -limit), limit).astype(held_as)


def gaussian_with(rng, extent, deviation, bound, shards, heavy, held_as=jnp.bfloat16):
    entries = deviation * jax.random.normal(rng, extent, jnp.float32)
    if shards:
        entries = entries * level_of(rng, extent, shards, -0.22, 0.18)
    return jnp.clip(with_spikes(entries, jax.random.fold_in(rng, 3), *heavy), -bound, bound).astype(held_as)


def setup_inputs(seed: int = 0) -> dict:
    seeds = jax.random.split(jax.random.key(seed), 7)
    tokens = gaussian_with(seeds[0], (TOKENS, D), 1.0, 6.0, ((0, 16), (1, 16)), (0, 1, 16, 2.0))
    cotangent = gaussian_with(seeds[1], (TOKENS, D), 1.0, 6.0, ((0, 16), (1, 16)), (0, 1, 16, 2.0))
    prefix = draw_prefix(jax.random.fold_in(seeds[6], 71), 0)
    gate_weight = scatter_about(seeds[3], (D, FF), D ** -0.5, 0.125, ((0, 16), (1, 16)))
    up_weight = scatter_about(seeds[4], (D, FF), D ** -0.5, 0.125, ((0, 16), (1, 16)))
    down_weight = scatter_about(seeds[5], (FF, D), FF ** -0.5, 0.046875, ((0, 16), (1, 16)))
    return {"tokens": tokens, "cotangent": cotangent, "prefix": prefix, "gate_weight": gate_weight, "up_weight": up_weight, "down_weight": down_weight}


def local_terms(inputs, cotangent_rows, keep_mask, gate_full, up_full, down_full):
    gate_pre = jnp.dot(inputs, gate_full, preferred_element_type=jnp.float32)
    up_pre = jnp.dot(inputs, up_full, preferred_element_type=jnp.float32)
    gate_sig = jax.nn.sigmoid(gate_pre)
    gate_act = gate_pre * gate_sig
    hidden = jnp.where(keep_mask, gate_act * up_pre, 0.0).astype(jnp.bfloat16)
    grad_hidden = lax.dot_general(cotangent_rows, down_full, (((1,), (1,)), ((), ())), preferred_element_type=jnp.float32)
    grad_gate = jnp.where(keep_mask, grad_hidden * up_pre * gate_sig * (1.0 + gate_pre * (1.0 - gate_sig)), 0.0).astype(jnp.bfloat16)
    grad_upper = jnp.where(keep_mask, grad_hidden * gate_act, 0.0).astype(jnp.bfloat16)
    return (hidden, grad_gate, grad_upper)

def rounded(values):
    return lax.optimization_barrier(values.astype(jnp.bfloat16)).astype(jnp.float32)

def reference(tokens, cotangent, prefix, gate_weight, up_weight, down_weight):
    grad_scale = 1.0 / math.sqrt(TOKENS)
    unit_ids = jnp.arange(FF, dtype=jnp.int32)
    limits = jnp.repeat(prefix, GROUP).reshape(N_DP, TOK_DEV)
    in_blocks = tokens.reshape(N_DP, TOK_DEV, D)
    cot_blocks = cotangent.reshape(N_DP, TOK_DEV, D)
    contract_rows = (((0,), (0,)), ((), ()))

    def per_block(carry, operands):
        sum_gate, sum_up, sum_down = carry
        inputs, cotangent_rows, limit_rows = operands
        keep_mask = unit_ids[None, :] < limit_rows[:, None]
        hidden, grad_gate, grad_upper = local_terms(inputs, cotangent_rows, keep_mask, gate_weight, up_weight, down_weight)
        mixed = jnp.dot(hidden, down_weight, preferred_element_type=jnp.float32).astype(jnp.bfloat16)
        back_gate = lax.dot_general(grad_gate, gate_weight, (((1,), (1,)), ((), ())), preferred_element_type=jnp.float32)
        back_up = lax.dot_general(grad_upper, up_weight, (((1,), (1,)), ((), ())), preferred_element_type=jnp.float32)
        input_grad = (back_gate + back_up).astype(jnp.bfloat16)
        term_gate = rounded(lax.dot_general(inputs, grad_gate, contract_rows, preferred_element_type=jnp.float32) * grad_scale)
        term_up = rounded(lax.dot_general(inputs, grad_upper, contract_rows, preferred_element_type=jnp.float32) * grad_scale)
        term_down = rounded(lax.dot_general(hidden, cotangent_rows, contract_rows, preferred_element_type=jnp.float32) * grad_scale)
        return ((sum_gate + term_gate, sum_up + term_up, sum_down + term_down), (mixed, input_grad))
    start = (jnp.zeros((D, FF), jnp.float32), jnp.zeros((D, FF), jnp.float32), jnp.zeros((FF, D), jnp.float32))
    sums, outputs = lax.scan(per_block, start, (in_blocks, cot_blocks, limits))
    mixed = outputs[0].reshape(TOKENS, D)
    input_grad = outputs[1].reshape(TOKENS, D)
    return (mixed, input_grad, sums[0].astype(jnp.bfloat16), sums[1].astype(jnp.bfloat16), sums[2].astype(jnp.bfloat16))
```

```python
import math

import jax
import jax.numpy as jnp
from jax import lax
from jax.experimental import pallas as pl
from jax.experimental.pallas import tpu as pltpu
from jax.sharding import Mesh
from jax.sharding import PartitionSpec as P


D = 2048
TOK = 6144
BF = jnp.bfloat16
F32 = jnp.float32
HALF = 192
ROWS = 768
UNITS = 512
OFFS = (0, 1, -1, 2)
ZOFFS = (0, 1, -1, 2, -2, 3, -3, 4)
PARAMS = dict(vmem_limit_bytes=44 * 1024 * 1024)
ANY = pl.BlockSpec(memory_space=pl.ANY)
SMEM = pl.BlockSpec(memory_space=pltpu.SMEM)


def shift(value, axis, by):
    return lax.ppermute(value, axis, [(i, (i + by) % 4) for i in range(4)])


def shift_z(value, by):
    pairs = []
    for z in range(8):
        to = (z + by) % 8
        pairs.append(((z % 4) * 2 + z // 4, (to % 4) * 2 + to // 4))
    return lax.ppermute(value, ("zl", "zh"), pairs)


def swap(value):
    return lax.ppermute(value, "c", [(0, 1), (1, 0)])


def run_copies(copies, sems, first=0):
    started = []
    for n, (src, dst) in enumerate(copies):
        copy = pltpu.make_async_copy(src, dst, sems.at[first + n])
        copy.start()
        started.append(copy)
    return started


def wait_all(started):
    for copy in started:
        copy.wait()


def spot(value, step):
    return pl.ds(pl.multiple_of(value * step, step), step)


def cost(flops, size):
    return pl.CostEstimate(flops=int(flops), bytes_accessed=int(size), transcendentals=0)


def shape(*dims):
    return jax.ShapeDtypeStruct(dims, BF)


def pack_kernel(co, gate, up, down, *rest):
    outs, sems = rest[:3], rest[3]
    zl = co[1]
    copies = []
    for out, off in zip(outs, OFFS[1:]):
        to = lax.rem(zl + off + 4, 4)
        copies.append((gate.at[:, spot(to, 256)], out.at[:, pl.ds(0, 256)]))
        copies.append((up.at[:, spot(to, 256)], out.at[:, pl.ds(256, 256)]))
        for h in range(2):
            copies.append((down.at[spot(to * 2 + h, 128), :], out.at[:, pl.ds(512 + 128 * h, 128)]))
    wait_all(run_copies(copies, sems))


def place_kernel(co, gate, up, down, *rest):
    pieces, out, sems = rest[:3], rest[3], rest[4]
    zl = co[1]
    copies = [
        (gate.at[:, spot(zl, 256)], out.at[spot(zl, 128), pl.ds(0, 256)]),
        (up.at[:, spot(zl, 256)], out.at[spot(zl, 128), pl.ds(256, 256)]),
        (down.at[spot(zl, 256), :], out.at[pl.ds(512, 256), spot(zl, 128)]),
    ]
    for piece, off in zip(pieces, OFFS[1:]):
        at = lax.rem(zl - off + 4, 4)
        copies.append((piece.at[:, pl.ds(0, 512)], out.at[spot(at, 128), :]))
        for h in range(2):
            copies.append(
                (piece.at[:, pl.ds(512 + 128 * h, 128)], out.at[pl.ds(512 + 128 * h, 128), spot(at, 128)])
            )
    wait_all(run_copies(copies, sems))


def pack_back_kernel(co, total, *rest):
    outs, sems = rest[:3], rest[3]
    zl = co[1]
    copies = []
    for out, off in zip(outs, OFFS[1:]):
        to = lax.rem(zl + off + 4, 4)
        copies.append((total.at[spot(to, 128), :], out.at[:, pl.ds(0, 512)]))
        for h in range(2):
            copies.append(
                (total.at[pl.ds(512 + 128 * h, 128), spot(to, 128)], out.at[:, pl.ds(512 + 128 * h, 128)])
            )
    wait_all(run_copies(copies, sems))


def place_back_kernel(co, total, *rest):
    pieces, (gate, up, down), sems = rest[:3], rest[3:6], rest[6]
    zl = co[1]
    copies = [
        (total.at[spot(zl, 128), pl.ds(0, 256)], gate.at[:, spot(zl, 256)]),
        (total.at[spot(zl, 128), pl.ds(256, 256)], up.at[:, spot(zl, 256)]),
        (total.at[pl.ds(512, 256), spot(zl, 128)], down.at[spot(zl, 256), :]),
    ]
    for piece, off in zip(pieces, OFFS[1:]):
        at = lax.rem(zl - off + 4, 4)
        copies.append((piece.at[:, pl.ds(0, 256)], gate.at[:, spot(at, 256)]))
        copies.append((piece.at[:, pl.ds(256, 256)], up.at[:, spot(at, 256)]))
        for h in range(2):
            copies.append((piece.at[:, pl.ds(512 + 128 * h, 128)], down.at[spot(at * 2 + h, 128), :]))
    wait_all(run_copies(copies, sems))


def move(kernel, count, co, *args, out_shape):
    size = sum(a.size for a in args) * 2
    return pl.pallas_call(
        kernel,
        out_shape=out_shape,
        in_specs=[SMEM] + [ANY] * len(args),
        out_specs=jax.tree.map(lambda _: ANY, out_shape),
        scratch_shapes=[pltpu.SemaphoreType.DMA((count,))],
        cost_estimate=cost(0, size),
    )(co, *args)


def weight_copies(co, own, other, wide, down):
    x = co[0]
    gate_up, downs = [], []
    for half, group in enumerate((own, other)):
        for piece, off in zip(group, OFFS):
            at = lax.rem(x - off + 4, 4)
            if wide is not None:
                for part in range(2):
                    gate_up.append(
                        (
                            piece.at[pl.ds(0, 512), pl.ds(256 * part, 256)],
                            wide.at[spot(at, 512), pl.ds(512 * part + 256 * half, 256)],
                        )
                    )
            if down is not None:
                downs.append((piece.at[pl.ds(512, 256), :], down.at[pl.ds(256 * half, 256), spot(at, 512)]))
    return gate_up, downs


def token_copies(co, pieces, whole):
    y, z = co[2], co[5]
    copies = []
    for n, off in enumerate(ZOFFS):
        at = lax.rem(z - off + 8, 8)
        for o, y_off in enumerate(OFFS):
            ys = lax.rem(y - y_off + 4, 4)
            if n < 7:
                src = pieces[n].at[pl.ds(o * HALF, HALF), :]
            else:
                src = pieces[7 + o // 2].at[pl.ds((o % 2) * HALF, HALF), :]
            copies.append((src, whole.at[spot(lax.rem(at, 4), HALF), spot(ys * 2 + at // 4, 256)]))
    return copies


def cot_copies(co, pieces, whole):
    y, z = co[2], co[5]
    copies = []
    for o, y_off in enumerate(OFFS):
        ys = lax.rem(y - y_off + 4, 4)
        for n, off in enumerate(ZOFFS):
            at = lax.rem(z - off + 8, 8)
            src = pieces[o].at[pl.ds(n * HALF, HALF), :]
            copies.append((src, whole.at[spot(lax.rem(at, 4), HALF), spot(ys * 2 + at // 4, 256)]))
    return copies


NN = (((1,), (0,)), ((), ()))
NT = (((1,), (1,)), ((), ()))


def dot(a, b, dims):
    return lax.dot_general(a, b, dims, preferred_element_type=F32)


def hidden_kernel(co, *refs):
    tok_in, cot_in, w_own, w_other = refs[:9], refs[9:13], refs[13:17], refs[17:21]
    hid_out, grads_out, mixed_out = refs[21], refs[22], refs[23:32]
    tok, cot, wide, down, hid, grads, mixed, limits, sems = refs[32:]
    c, zl, y, zh, z = co[4], co[1], co[2], co[3], co[5]
    gate_up, downs = weight_copies(co, w_own, w_other, wide, down)
    limit_copies = []
    for n, off in enumerate(ZOFFS[:7]):
        if off in (0, 1, -1, 2):
            at = lax.rem(z - off + 8, 4)
            limit_copies.append((tok_in[n].at[pl.ds(ROWS, 16), :], limits.at[spot(at, 16), :]))
    early = run_copies(gate_up + token_copies(co, tok_in, tok) + limit_copies, sems)
    late = run_copies(cot_copies(co, cot_in, cot) + downs, sems, len(early))
    wait_all(early)
    wait_all(late)
    split = 128 - 64 * c
    for half in range(2):
        core = c if half == 0 else 1 - c
        first = ((y * 2 + zh) * 2 + core) * 1024 + zl * 256
        col = pl.ds(256 * half, 256)
        up_col = pl.ds(512 + 256 * half, 256)
        gate_pre = dot(tok[...], wide[:, col], NN)
        up_pre = dot(tok[...], wide[:, up_col], NN)
        grad_hidden = dot(cot[...], down[col, :], NT)
        unit = (first + lax.broadcasted_iota(jnp.int32, (HALF, 256), 1)).astype(F32)
        row = lax.broadcasted_iota(jnp.int32, (HALF, 256), 0)
        for block in range(4):
            rows = slice(block * HALF, block * HALF + HALF)
            low = limits[16 * block : 16 * block + 1, :].astype(F32)
            high = limits[16 * block + 1 : 16 * block + 2, :].astype(F32)
            keep = unit < jnp.where(row < split, low, high)
            g, u, gh = gate_pre[rows], up_pre[rows], grad_hidden[rows]
            sig = jax.nn.sigmoid(g)
            act = g * sig
            hid[rows, col] = jnp.where(keep, act * u, 0.0).astype(BF)
            grads[rows, col] = jnp.where(keep, gh * u * sig * (1.0 + g * (1.0 - sig)), 0.0).astype(BF)
            grads[rows, up_col] = jnp.where(keep, gh * act, 0.0).astype(BF)
    first_sem = len(early) + len(late)
    kept = run_copies([(hid, hid_out), (grads, grads_out)], sems, first_sem)

    @pl.loop(0, 8)
    def _(n):
        block = spot(n, 256)
        mixed[:, block] = dot(hid[...], down[:, block], NN).astype(BF)

    copies = []
    for n, off in enumerate(ZOFFS):
        to = lax.rem(z + off + 8, 8)
        for o, y_off in enumerate(OFFS):
            yd = lax.rem(y + y_off + 4, 4)
            src = mixed.at[spot(lax.rem(to, 4), HALF), spot(yd * 2 + to // 4, 256)]
            if n < 7:
                dst = mixed_out[n].at[pl.ds(o * HALF, HALF), :]
            else:
                dst = mixed_out[7 + o // 2].at[pl.ds((o % 2) * HALF, HALF), :]
            copies.append((src, dst))
    wait_all(run_copies(copies, sems, first_sem + 2))
    wait_all(kept)


def hidden_call(co, tok_in, cot_in, w_own, w_other):
    args = (*tok_in, *cot_in, *w_own, *w_other)
    outs = (
        [shape(ROWS, UNITS), shape(ROWS, 2 * UNITS)]
        + [shape(ROWS, 256) for _ in range(7)]
        + [shape(ROWS // 2, 256) for _ in range(2)]
    )
    out = pl.pallas_call(
        hidden_kernel,
        out_shape=outs,
        in_specs=[SMEM] + [ANY] * len(args),
        out_specs=[ANY] * len(outs),
        scratch_shapes=[
            pltpu.VMEM((ROWS, D), BF),
            pltpu.VMEM((ROWS, D), BF),
            pltpu.VMEM((D, 2 * UNITS), BF),
            pltpu.VMEM((UNITS, D), BF),
            pltpu.VMEM((ROWS, UNITS), BF),
            pltpu.VMEM((ROWS, 2 * UNITS), BF),
            pltpu.VMEM((ROWS, D), BF),
            pltpu.VMEM((64, 256), BF),
            pltpu.SemaphoreType.DMA((128 + 32,)),
        ],
        compiler_params=pltpu.CompilerParams(**PARAMS),
        cost_estimate=cost(8 * ROWS * D * UNITS, 18e6),
    )(co, *args)
    return out[0], out[1], out[2:]


def weight_grad_kernel(co, *refs):
    hid_in, grads_in, tok_in, cot_in = refs[0], refs[1], refs[2:11], refs[11:15]
    own_out, other_out = refs[15:19], refs[19:23]
    tok, cot, hid, grads, wide, down, hid_t, sems = refs[23:]
    scale = 1.0 / math.sqrt(TOK)
    first = run_copies([(grads_in, grads)] + token_copies(co, tok_in, tok), sems)
    second = run_copies([(hid_in, hid)] + cot_copies(co, cot_in, cot), sems, len(first))
    wait_all(first)
    wait_all(second)

    @pl.loop(0, 8)
    def _(n):
        block = spot(n, 256)
        turned = tok[:, block].T
        wide[block, :] = (dot(turned, grads[...], NN) * scale).astype(BF)

    hid_t[...] = hid[...].T

    @pl.loop(0, 8)
    def _(n):
        block = spot(n, 256)
        down[:, block] = (dot(hid_t[...], cot[:, block], NN) * scale).astype(BF)

    x = co[0]
    copies = []
    for half, group in enumerate((own_out, other_out)):
        for piece, off in zip(group, OFFS):
            to = lax.rem(x + off + 4, 4)
            for part in range(2):
                copies.append(
                    (
                        wide.at[spot(to, 512), pl.ds(512 * part + 256 * half, 256)],
                        piece.at[pl.ds(0, 512), pl.ds(256 * part, 256)],
                    )
                )
            copies.append((down.at[pl.ds(256 * half, 256), spot(to, 512)], piece.at[pl.ds(512, 256), :]))
    wait_all(run_copies(copies, sems, len(first) + len(second)))


def weight_grad_call(co, hid, grads, tok_in, cot_in):
    args = (hid, grads, *tok_in, *cot_in)
    out = pl.pallas_call(
        weight_grad_kernel,
        out_shape=[shape(768, 512) for _ in range(8)],
        in_specs=[SMEM] + [ANY] * len(args),
        out_specs=[ANY] * 8,
        scratch_shapes=[
            pltpu.VMEM((ROWS, D), BF),
            pltpu.VMEM((ROWS, D), BF),
            pltpu.VMEM((ROWS, UNITS), BF),
            pltpu.VMEM((ROWS, 2 * UNITS), BF),
            pltpu.VMEM((D, 2 * UNITS), BF),
            pltpu.VMEM((UNITS, D), BF),
            pltpu.VMEM((UNITS, ROWS), BF),
            pltpu.SemaphoreType.DMA((96,)),
        ],
        compiler_params=pltpu.CompilerParams(**PARAMS),
        cost_estimate=cost(6 * ROWS * D * UNITS, 15e6),
    )(co, *args)
    return out[:4], out[4:]


def input_grad_kernel(co, *refs):
    grads_in, w_own, w_other, outs = refs[0], refs[1:5], refs[5:9], refs[9:13]
    grads, wide, result, sems = refs[13:]
    gate_up, _ = weight_copies(co, w_own, w_other, wide, None)
    started = run_copies([(grads_in, grads)] + gate_up, sems)
    wait_all(started)

    @pl.loop(0, 8)
    def _(n):
        block = spot(n, 256)
        result[:, block] = dot(grads[...], wide[block, :], NT).astype(BF)

    y, z = co[2], co[5]
    copies = []
    for o, y_off in enumerate(OFFS):
        yd = lax.rem(y + y_off + 4, 4)
        for n, off in enumerate(ZOFFS):
            to = lax.rem(z + off + 8, 8)
            src = result.at[spot(lax.rem(to, 4), HALF), spot(yd * 2 + to // 4, 256)]
            copies.append((src, outs[o].at[pl.ds(n * HALF, HALF), :]))
    wait_all(run_copies(copies, sems, len(started)))


def input_grad_call(co, grads, w_own, w_other):
    args = (grads, *w_own, *w_other)
    return pl.pallas_call(
        input_grad_kernel,
        out_shape=[shape(8 * HALF, 256) for _ in range(4)],
        in_specs=[SMEM] + [ANY] * len(args),
        out_specs=[ANY] * 4,
        scratch_shapes=[
            pltpu.VMEM((ROWS, 2 * UNITS), BF),
            pltpu.VMEM((D, 2 * UNITS), BF),
            pltpu.VMEM((ROWS, D), BF),
            pltpu.SemaphoreType.DMA((64,)),
        ],
        compiler_params=pltpu.CompilerParams(**PARAMS),
        cost_estimate=cost(4 * ROWS * D * UNITS, 10e6),
    )(co, *args)


def gather_z(value, last_rows):
    up = down = value
    pieces = [value]
    for _ in range(3):
        up, down = shift_z(up, 1), shift_z(down, -1)
        pieces += [up, down]
    half = last_rows // 2
    return pieces + [shift_z(up[:half], 1), shift_z(down[half:last_rows], -1)]


def add(*terms):
    total = terms[0].astype(F32)
    for term in terms[1:]:
        total = total + term.astype(F32)
    return total.astype(BF)


def scatter_z(pieces):
    up, down = shift_z(pieces[7], 1), shift_z(pieces[8], -1)
    half = up.shape[0]
    up = jnp.concatenate([add(pieces[5][:half], up), pieces[5][half:]])
    down = jnp.concatenate([pieces[6][:half], add(pieces[6][half:], down)])
    up, down = shift_z(up, 1), shift_z(down, -1)
    up, down = add(pieces[3], up), add(pieces[4], down)
    up, down = shift_z(up, 1), shift_z(down, -1)
    up, down = add(pieces[1], up), add(pieces[2], down)
    up, down = shift_z(up, 1), shift_z(down, -1)
    return add(pieces[0], up, down)


def split_cores(value, c):
    away = lax.dynamic_slice_in_dim(value, (1 - c) * HALF, HALF, 0)
    kept = lax.dynamic_slice_in_dim(value, c * HALF, HALF, 0)
    got = swap(away)
    return jnp.where(c == 0, jnp.concatenate([kept, got], 1), jnp.concatenate([got, kept], 1))


def join_cores(value, c):
    away = lax.dynamic_slice_in_dim(value, (1 - c) * 128, 128, 1)
    kept = lax.dynamic_slice_in_dim(value, c * 128, 128, 1)
    got = swap(away)
    return jnp.where(c == 0, jnp.concatenate([kept, got], 0), jnp.concatenate([got, kept], 0))


def local(tokens, cotangent, prefix, gate_weight, up_weight, down_weight):
    x, zl, y, zh, c = (lax.axis_index(a) for a in ("x", "zl", "y", "zh", "c"))
    co = jnp.stack([x, zl, y, zh, c, zh * 4 + zl, x, x]).astype(jnp.int32)

    sent = move(
        pack_kernel, 12, co, gate_weight, up_weight, down_weight, out_shape=[shape(128, 768) for _ in range(3)]
    )
    tok = split_cores(tokens, c)
    cot = split_cores(cotangent, c)
    got = [shift(v, "zl", off) for v, off in zip(sent, OFFS[1:])]

    mine = lax.dynamic_slice_in_dim(prefix, c, 2).astype(BF)
    limits = jnp.broadcast_to(jnp.pad(mine, (0, 14))[:, None], (16, 256))
    tok_y = [tok] + [shift(tok, "y", off) for off in OFFS[1:]]
    tok_in = gather_z(jnp.concatenate(tok_y + [limits]), ROWS)
    cot_z = gather_z(cot, HALF)
    cot_own = jnp.concatenate(cot_z)
    cot_in = [cot_own] + [shift(cot_own, "y", off) for off in OFFS[1:]]

    placed = move(
        place_kernel, 12, co, gate_weight, up_weight, down_weight, *got, out_shape=shape(768, 512)
    )
    w_own = [placed] + [shift(placed, "x", off) for off in OFFS[1:]]
    w_other = [swap(v) for v in w_own]

    hid, grads, mixed_terms = hidden_call(co, tok_in, cot_in, w_own, w_other)
    own_terms, other_terms = weight_grad_call(co, hid, grads, tok_in, cot_in)
    back_terms = input_grad_call(co, grads, w_own, w_other)

    mixed_z = scatter_z(mixed_terms)
    parts = [mixed_z[o * HALF : (o + 1) * HALF] for o in range(4)]
    mixed = join_cores(add(parts[0], *[shift(p, "y", off) for p, off in zip(parts[1:], OFFS[1:])]), c)

    chip_terms = [add(a, swap(b)) for a, b in zip(own_terms, other_terms)]
    total = add(chip_terms[0], *[shift(p, "x", off) for p, off in zip(chip_terms[1:], OFFS[1:])])

    back_y = add(back_terms[0], *[shift(p, "y", off) for p, off in zip(back_terms[1:], OFFS[1:])])
    pieces = [back_y[n * HALF : (n + 1) * HALF] for n in range(8)]
    pieces = pieces[:7] + [pieces[7][: HALF // 2], pieces[7][HALF // 2 :]]
    input_grad = join_cores(scatter_z(pieces), c)

    sent = move(pack_back_kernel, 9, co, total, out_shape=[shape(128, 768) for _ in range(3)])
    got = [shift(v, "zl", off) for v, off in zip(sent, OFFS[1:])]
    gate_grad, up_grad, down_grad = move(
        place_back_kernel,
        15,
        co,
        total,
        *got,
        out_shape=[shape(128, 1024), shape(128, 1024), shape(1024, 128)],
    )
    return mixed, input_grad, gate_grad, up_grad, down_grad


def solution(mesh):
    fine = Mesh(mesh.devices.reshape(4, 4, 4, 2, 2), ("x", "zl", "y", "zh", "c"))
    rows, columns = ("x", "zl"), ("y", "zh", "c")
    return jax.shard_map(
        local,
        mesh=fine,
        in_specs=(
            P(rows, columns),
            P(rows, columns),
            P(rows),
            P(rows, columns),
            P(rows, columns),
            P(columns, rows),
        ),
        out_specs=(
            P(rows, columns),
            P(rows, columns),
            P(rows, columns),
            P(rows, columns),
            P(columns, rows),
        ),
        check_vma=False,
    )
```

```python
import math

import jax
import jax.numpy as jnp
from jax import lax
from jax.experimental import pallas as pl
from jax.experimental.pallas import tpu as pltpu
from jax.sharding import Mesh
from jax.sharding import PartitionSpec as P


D = 2048
TOK = 6144
BF = jnp.bfloat16
F32 = jnp.float32
HALF = 192
ROWS = 768
UNITS = 512
OFFS = (0, 1, -1, 2)
ZOFFS = (0, 1, -1, 2, -2, 3, -3, 4)
VMEM_LIMIT = 58 * 1024 * 1024
ANY = pl.BlockSpec(memory_space=pl.ANY)
VMEM = pl.BlockSpec(memory_space=pltpu.VMEM)
SMEM = pl.BlockSpec(memory_space=pltpu.SMEM)


def shift(value, axis, by):
    return lax.ppermute(value, axis, [(i, (i + by) % 4) for i in range(4)])


def shift_z(value, by):
    pairs = []
    for z in range(8):
        to = (z + by) % 8
        pairs.append(((z % 4) * 2 + z // 4, (to % 4) * 2 + to // 4))
    return lax.ppermute(value, ("zl", "zh"), pairs)


def swap(value):
    return lax.ppermute(value, "c", [(0, 1), (1, 0)])


def run_copies(copies, sems, first=0):
    started = []
    for n, (src, dst) in enumerate(copies):
        copy = pltpu.make_async_copy(src, dst, sems.at[first + n])
        copy.start()
        started.append(copy)
    return started


def wait_all(started):
    for copy in started:
        copy.wait()


def spot(value, step):
    return pl.ds(pl.multiple_of(value * step, step), step)


def cost(flops, size):
    return pl.CostEstimate(flops=int(flops), bytes_accessed=int(size), transcendentals=0)


def shape(*dims):
    return jax.ShapeDtypeStruct(dims, BF)


def pack_kernel(co, gate, up, down, *outs):
    zl = co[1]
    for out, off in zip(outs, OFFS[1:]):
        to = lax.rem(zl + off + 4, 4)
        out[:, 0:256] = gate[:, spot(to, 256)]
        out[:, 256:512] = up[:, spot(to, 256)]
        for h in range(2):
            out[:, 512 + 128 * h : 640 + 128 * h] = down[spot(to * 2 + h, 128), :]


def place_kernel(co, gate, up, down, *rest):
    pieces, out = rest[:3], rest[3]
    zl = co[1]
    out[spot(zl, 128), 0:256] = gate[:, spot(zl, 256)]
    out[spot(zl, 128), 256:512] = up[:, spot(zl, 256)]
    out[512:768, spot(zl, 128)] = down[spot(zl, 256), :]
    for piece, off in zip(pieces, OFFS[1:]):
        at = lax.rem(zl - off + 4, 4)
        out[spot(at, 128), :] = piece[:, 0:512]
        for h in range(2):
            out[512 + 128 * h : 640 + 128 * h, spot(at, 128)] = piece[:, 512 + 128 * h : 640 + 128 * h]


def pack_back_kernel(co, total, *outs):
    zl = co[1]
    for out, off in zip(outs, OFFS[1:]):
        to = lax.rem(zl + off + 4, 4)
        out[:, 0:512] = total[spot(to, 128), :]
        for h in range(2):
            out[:, 512 + 128 * h : 640 + 128 * h] = total[512 + 128 * h : 640 + 128 * h, spot(to, 128)]


def place_back_kernel(co, total, *rest):
    pieces, (gate, up, down) = rest[:3], rest[3:6]
    zl = co[1]
    gate[:, spot(zl, 256)] = total[spot(zl, 128), 0:256]
    up[:, spot(zl, 256)] = total[spot(zl, 128), 256:512]
    down[spot(zl, 256), :] = total[512:768, spot(zl, 128)]
    for piece, off in zip(pieces, OFFS[1:]):
        at = lax.rem(zl - off + 4, 4)
        gate[:, spot(at, 256)] = piece[:, 0:256]
        up[:, spot(at, 256)] = piece[:, 256:512]
        for h in range(2):
            down[spot(at * 2 + h, 128), :] = piece[:, 512 + 128 * h : 640 + 128 * h]


def move(kernel, co, *args, out_shape):
    size = sum(a.size for a in args) * 2
    return pl.pallas_call(
        kernel,
        out_shape=out_shape,
        in_specs=[SMEM] + [VMEM] * len(args),
        out_specs=jax.tree.map(lambda _: VMEM, out_shape),
        cost_estimate=cost(0, size),
    )(co, *args)


def rows_of(pieces, o, first, count):
    if o < 3:
        return pieces[o].at[pl.ds(first, count), :]
    half = pieces[3].shape[0]
    if first < half:
        return pieces[3].at[pl.ds(first, count), :]
    return pieces[4].at[pl.ds(first - half, count), :]


def weight_copies(co, way, own, other, wide, down):
    x = co[0]
    gate_up, downs = [], []
    for half, group in enumerate((own, other)):
        for o, off in enumerate(OFFS):
            at = lax.rem(x - way * off + 4, 4)
            for first, count in ((0, 512),) if o < 3 else ((0, 384), (384, 128)):
                piece = rows_of(group, o, first, count)
                for part in range(2):
                    rows = pl.ds(pl.multiple_of(at * 512 + first, 128), count)
                    place = wide.at[rows, pl.ds(512 * part + 256 * half, 256)]
                    gate_up.append((piece.at[:, pl.ds(256 * part, 256)], place)[::way])
            place = down.at[pl.ds(256 * half, 256), spot(at, 512)]
            downs.append((rows_of(group, o, 512, 256), place)[::way])
    return gate_up, downs


def whole_spot(y, z, whole):
    return whole.at[spot(lax.rem(z, 4), HALF), spot(y * 2 + z // 4, 256)]


def z_first_copies(co, way, pieces, whole):
    copies = []
    for n, off in enumerate(ZOFFS):
        at = lax.rem(co[5] - way * off + 8, 8)
        for o, y_off in enumerate(OFFS):
            piece = pieces[n] if n < 7 else pieces[7 + o // 2]
            src = piece.at[pl.ds((o if n < 7 else o % 2) * HALF, HALF), :]
            copies.append((src, whole_spot(lax.rem(co[2] - way * y_off + 4, 4), at, whole))[::way])
    return copies


def y_first_copies(co, way, pieces, whole):
    copies = []
    for o, y_off in enumerate(OFFS):
        y = lax.rem(co[2] - way * y_off + 4, 4)
        for n, off in enumerate(ZOFFS):
            src = rows_of(pieces, o, n * HALF, HALF)
            copies.append((src, whole_spot(y, lax.rem(co[5] - way * off + 8, 8), whole))[::way])
    return copies


NN = (((1,), (0,)), ((), ()))
NT = (((1,), (1,)), ((), ()))


def dot(a, b, dims):
    return lax.dot_general(a, b, dims, preferred_element_type=F32)


def call(kernel, co, args, outs, scratch, sems, cost_estimate):
    return pl.pallas_call(
        kernel,
        out_shape=outs,
        in_specs=[SMEM] + [ANY] * len(args),
        out_specs=[ANY] * len(outs),
        scratch_shapes=[pltpu.VMEM(s, BF) for s in scratch] + [pltpu.SemaphoreType.DMA((sems,))],
        compiler_params=pltpu.CompilerParams(vmem_limit_bytes=VMEM_LIMIT),
        cost_estimate=cost_estimate,
    )(co, *args)


def hidden_kernel(co, *refs):
    tok_in, cot_in, w_own, w_other = refs[:9], refs[9:14], refs[14:19], refs[19:24]
    hid_out, grads_out, mixed_out, back_out = refs[24], refs[25], refs[26:35], refs[35:40]
    tok, cot, wide, down, hid, grads, mixed, back, limits, sems = refs[40:]
    zl, y, zh, c, z = co[1], co[2], co[3], co[4], co[5]
    gate_up, downs = weight_copies(co, 1, w_own, w_other, wide, down)
    limit_copies = []
    for n, off in enumerate(ZOFFS[:4]):
        at = lax.rem(z - off + 8, 4)
        limit_copies.append((tok_in[n].at[pl.ds(ROWS, 16), :], limits.at[spot(at, 16), :]))
    early = run_copies(gate_up + z_first_copies(co, 1, tok_in, tok) + limit_copies, sems)
    late = run_copies(y_first_copies(co, 1, cot_in, cot) + downs, sems, len(early))
    used = len(early) + len(late)
    wait_all(early)
    wait_all(late)
    split = 128 - 64 * c

    @pl.loop(0, 2)
    def _(m):
        part = spot(m, 2 * HALF)
        pre = dot(tok[part, :], wide[...], NN)
        grad_hidden = dot(cot[part, :], down[...], NT)
        for half in range(2):
            core = c if half == 0 else 1 - c
            first = ((y * 2 + zh) * 2 + core) * 1024 + zl * 256
            unit = (first + lax.broadcasted_iota(jnp.int32, (HALF, 256), 1)).astype(F32)
            row = lax.broadcasted_iota(jnp.int32, (HALF, 256), 0)
            for block in range(2):
                limit = limits[spot(2 * m + block, 16), :].astype(F32)
                keep = unit < jnp.where(row < split, limit[0:1], limit[1:2])
                near = slice(block * HALF, block * HALF + HALF)
                rows = spot(2 * m + block, HALF)
                g = pre[near, 256 * half : 256 * half + 256]
                u = pre[near, 512 + 256 * half : 768 + 256 * half]
                gh = grad_hidden[near, 256 * half : 256 * half + 256]
                sig = jax.nn.sigmoid(g)
                act = g * sig
                gate_part, up_part = pl.ds(256 * half, 256), pl.ds(512 + 256 * half, 256)
                hid[rows, gate_part] = jnp.where(keep, act * u, 0.0).astype(BF)
                grads[rows, gate_part] = jnp.where(
                    keep, gh * u * sig * (1.0 + g * (1.0 - sig)), 0.0
                ).astype(BF)
                grads[rows, up_part] = jnp.where(keep, gh * act, 0.0).astype(BF)

    kept = run_copies([(hid, hid_out), (grads, grads_out)], sems, used)

    @pl.loop(0, 3)
    def _(m):
        rows = spot(m, 256)
        mixed[rows, :] = dot(hid[rows, :], down[...], NN).astype(BF)

    kept += run_copies(z_first_copies(co, -1, mixed_out, mixed), sems, used + 2)

    @pl.loop(0, 3)
    def _(m):
        rows = spot(m, 256)
        back[rows, :] = dot(grads[rows, :], wide[...], NT).astype(BF)

    kept += run_copies(y_first_copies(co, -1, back_out, back), sems, used + 34)
    wait_all(kept)


def hidden_call(co, tok_in, cot_in, w_own, w_other):
    outs = [shape(ROWS, UNITS), shape(ROWS, 2 * UNITS)]
    outs += [shape(ROWS, 256) for _ in range(7)] + [shape(ROWS // 2, 256) for _ in range(2)]
    outs += [shape(8 * HALF, 256) for _ in range(3)] + [shape(4 * HALF, 256) for _ in range(2)]
    scratch = [(ROWS, D), (ROWS, D), (D, 2 * UNITS), (UNITS, D), (ROWS, UNITS), (ROWS, 2 * UNITS)]
    scratch += [(ROWS, D), (ROWS, D), (64, 256)]
    out = call(
        hidden_kernel,
        co,
        (*tok_in, *cot_in, *w_own, *w_other),
        outs,
        scratch,
        20 + 32 + 4 + 32 + 8 + 66,
        cost(12 * ROWS * D * UNITS, 22e6),
    )
    return out[0], out[1], out[2:11], out[11:]


def weight_grad_kernel(co, *refs):
    hid_in, grads_in, tok_in, cot_in = refs[0], refs[1], refs[2:11], refs[11:16]
    own_out, other_out = refs[16:21], refs[21:26]
    tok, cot, hid, grads, wide, down, sems = refs[26:]
    scale = 1.0 / math.sqrt(TOK)
    first = run_copies([(grads_in, grads)] + z_first_copies(co, 1, tok_in, tok), sems)
    second = run_copies([(hid_in, hid)] + y_first_copies(co, 1, cot_in, cot), sems, len(first))
    wait_all(first)

    @pl.loop(0, 8)
    def _(n):
        block = spot(n, 256)
        wide[block, :] = (dot(tok[:, block].T, grads[...], NN) * scale).astype(BF)

    wait_all(second)

    @pl.loop(0, 2)
    def _(n):
        block = spot(n, 256)
        down[block, :] = (dot(hid[:, block].T, cot[...], NN) * scale).astype(BF)

    gate_up, downs = weight_copies(co, -1, own_out, other_out, wide, down)
    wait_all(run_copies(gate_up + downs, sems, len(first) + len(second)))


def weight_grad_call(co, hid, grads, tok_in, cot_in):
    ring = [shape(768, 512) for _ in range(3)] + [shape(384, 512) for _ in range(2)]
    scratch = [(ROWS, D), (ROWS, D), (ROWS, UNITS), (ROWS, 2 * UNITS), (D, 2 * UNITS), (UNITS, D)]
    out = call(
        weight_grad_kernel,
        co,
        (hid, grads, *tok_in, *cot_in),
        ring + ring,
        scratch,
        66 + 28,
        cost(6 * ROWS * D * UNITS, 15e6),
    )
    return out[:5], out[5:]


def gather_4(value, axis):
    up, down = shift(value, axis, 1), shift(value, axis, -1)
    half = value.shape[0] // 2
    return [value, up, down, shift(up[:half], axis, 1), shift(down[half:], axis, -1)]


def gather_z(value, last_rows):
    up = down = value
    pieces = [value]
    for _ in range(3):
        up, down = shift_z(up, 1), shift_z(down, -1)
        pieces += [up, down]
    half = last_rows // 2
    return pieces + [shift_z(up[:half], 1), shift_z(down[half:last_rows], -1)]


def add(*terms):
    total = terms[0].astype(F32)
    for term in terms[1:]:
        total = total + term.astype(F32)
    return total.astype(BF)


def scatter_4(pieces, axis):
    up, down = shift(pieces[3], axis, 1), shift(pieces[4], axis, -1)
    half = up.shape[0]
    up = jnp.concatenate([add(pieces[1][:half], up), pieces[1][half:]])
    down = jnp.concatenate([pieces[2][:half], add(pieces[2][half:], down)])
    return add(pieces[0], shift(up, axis, 1), shift(down, axis, -1))


def scatter_z(pieces):
    up, down = shift_z(pieces[7], 1), shift_z(pieces[8], -1)
    half = up.shape[0]
    up = jnp.concatenate([add(pieces[5][:half], up), pieces[5][half:]])
    down = jnp.concatenate([pieces[6][:half], add(pieces[6][half:], down)])
    up, down = shift_z(up, 1), shift_z(down, -1)
    up, down = add(pieces[3], up), add(pieces[4], down)
    up, down = shift_z(up, 1), shift_z(down, -1)
    up, down = add(pieces[1], up), add(pieces[2], down)
    up, down = shift_z(up, 1), shift_z(down, -1)
    return add(pieces[0], up, down)


def split_cores(value, c):
    away = lax.dynamic_slice_in_dim(value, (1 - c) * HALF, HALF, 0)
    kept = lax.dynamic_slice_in_dim(value, c * HALF, HALF, 0)
    got = swap(away)
    return jnp.where(c == 0, jnp.concatenate([kept, got], 1), jnp.concatenate([got, kept], 1))


def join_cores(value, c):
    away = lax.dynamic_slice_in_dim(value, (1 - c) * 128, 128, 1)
    kept = lax.dynamic_slice_in_dim(value, c * 128, 128, 1)
    got = swap(away)
    return jnp.where(c == 0, jnp.concatenate([kept, got], 0), jnp.concatenate([got, kept], 0))


def local(tokens, cotangent, prefix, gate_weight, up_weight, down_weight):
    x, zl, y, zh, c = (lax.axis_index(a) for a in ("x", "zl", "y", "zh", "c"))
    co = jnp.stack([x, zl, y, zh, c, zh * 4 + zl, x, x]).astype(jnp.int32)

    sent = move(pack_kernel, co, gate_weight, up_weight, down_weight, out_shape=[shape(128, 768)] * 3)
    tok = split_cores(tokens, c)
    cot = split_cores(cotangent, c)
    got = [shift(v, "zl", off) for v, off in zip(sent, OFFS[1:])]

    mine = lax.dynamic_slice_in_dim(prefix, c, 2).astype(BF)
    limits = jnp.broadcast_to(jnp.pad(mine, (0, 14))[:, None], (16, 256))
    tok_y = [tok] + [shift(tok, "y", off) for off in OFFS[1:]]
    tok_in = gather_z(jnp.concatenate(tok_y + [limits]), ROWS)
    cot_in = gather_4(jnp.concatenate(gather_z(cot, HALF)), "y")

    placed = move(place_kernel, co, gate_weight, up_weight, down_weight, *got, out_shape=shape(768, 512))
    w_own = gather_4(placed, "x")
    w_other = [swap(v) for v in w_own]

    hid, grads, mixed_terms, back_terms = hidden_call(co, tok_in, cot_in, w_own, w_other)
    own_terms, other_terms = weight_grad_call(co, hid, grads, tok_in, cot_in)

    mixed_z = scatter_z(mixed_terms)
    parts = [mixed_z[o * HALF : (o + 1) * HALF] for o in range(4)]
    mixed = join_cores(add(parts[0], *[shift(p, "y", off) for p, off in zip(parts[1:], OFFS[1:])]), c)

    total = scatter_4([add(a, swap(b)) for a, b in zip(own_terms, other_terms)], "x")

    back_y = scatter_4(back_terms, "y")
    pieces = [back_y[n * HALF : (n + 1) * HALF] for n in range(8)]
    pieces = pieces[:7] + [pieces[7][: HALF // 2], pieces[7][HALF // 2 :]]
    input_grad = join_cores(scatter_z(pieces), c)

    sent = move(pack_back_kernel, co, total, out_shape=[shape(128, 768)] * 3)
    got = [shift(v, "zl", off) for v, off in zip(sent, OFFS[1:])]
    gate_grad, up_grad, down_grad = move(
        place_back_kernel, co, total, *got, out_shape=[shape(128, 1024), shape(128, 1024), shape(1024, 128)]
    )
    return mixed, input_grad, gate_grad, up_grad, down_grad


def solution(mesh):
    fine = Mesh(mesh.devices.reshape(4, 4, 4, 2, 2), ("x", "zl", "y", "zh", "c"))
    rows, columns = ("x", "zl"), ("y", "zh", "c")
    return jax.shard_map(
        local,
        mesh=fine,
        in_specs=(
            P(rows, columns),
            P(rows, columns),
            P(rows),
            P(rows, columns),
            P(rows, columns),
            P(columns, rows),
        ),
        out_specs=(
            P(rows, columns),
            P(rows, columns),
            P(rows, columns),
            P(rows, columns),
            P(columns, rows),
        ),
        check_vma=False,
    )
```

```python
import math

import jax
import jax.numpy as jnp
from jax import lax
from jax.experimental import pallas as pl
from jax.experimental.pallas import tpu as pltpu
from jax.sharding import Mesh
from jax.sharding import PartitionSpec as P


D = 2048
TOK = 6144
BF = jnp.bfloat16
F32 = jnp.float32
HALF = 192
ROWS = 768
UNITS = 512
OFFS = (0, 1, -1, 2)
ZOFFS = (0, 1, -1, 2, -2, 3, -3, 4)
VMEM_LIMIT = 58 * 1024 * 1024
ANY = pl.BlockSpec(memory_space=pl.ANY)
VMEM = pl.BlockSpec(memory_space=pltpu.VMEM)
SMEM = pl.BlockSpec(memory_space=pltpu.SMEM)


def shift(value, axis, by):
    return lax.ppermute(value, axis, [(i, (i + by) % 4) for i in range(4)])


def shift_z(value, by):
    pairs = []
    for z in range(8):
        to = (z + by) % 8
        pairs.append(((z % 4) * 2 + z // 4, (to % 4) * 2 + to // 4))
    return lax.ppermute(value, ("zl", "zh"), pairs)


def spin(value, axis):
    pairs = [(2 * i + c, (i + (1, -1)[c]) % 4 * 2 + c) for i in range(4) for c in range(2)]
    return lax.ppermute(value, (axis, "c"), pairs)


def together(*values):
    return lax.optimization_barrier(values)


def swap(value):
    return lax.ppermute(value, "c", [(0, 1), (1, 0)])


def run_copies(copies, sems, first=0):
    started = []
    for n, (src, dst) in enumerate(copies):
        copy = pltpu.make_async_copy(src, dst, sems.at[first + n])
        copy.start()
        started.append(copy)
    return started


def wait_all(started):
    for copy in started:
        copy.wait()


def spot(value, step):
    return pl.ds(pl.multiple_of(value * step, step), step)


def cost(flops, size):
    return pl.CostEstimate(flops=int(flops), bytes_accessed=int(size), transcendentals=0)


def shape(*dims):
    return jax.ShapeDtypeStruct(dims, BF)


def pack_kernel(co, gate, up, down, *outs):
    zl = co[1]
    for out, off in zip(outs, OFFS[1:]):
        to = lax.rem(zl + off + 4, 4)
        out[:, 0:256] = gate[:, spot(to, 256)]
        out[:, 256:512] = up[:, spot(to, 256)]
        for h in range(2):
            out[:, 512 + 128 * h : 640 + 128 * h] = down[spot(to * 2 + h, 128), :]


def place_kernel(co, gate, up, down, *rest):
    pieces, out = rest[:3], rest[3]
    zl = co[1]
    out[spot(zl, 128), 0:256] = gate[:, spot(zl, 256)]
    out[spot(zl, 128), 256:512] = up[:, spot(zl, 256)]
    out[512:768, spot(zl, 128)] = down[spot(zl, 256), :]
    for piece, off in zip(pieces, OFFS[1:]):
        at = lax.rem(zl - off + 4, 4)
        out[spot(at, 128), :] = piece[:, 0:512]
        for h in range(2):
            out[512 + 128 * h : 640 + 128 * h, spot(at, 128)] = piece[:, 512 + 128 * h : 640 + 128 * h]


def pack_back_kernel(co, total, *outs):
    zl = co[1]
    for out, off in zip(outs, OFFS[1:]):
        to = lax.rem(zl + off + 4, 4)
        out[:, 0:512] = total[spot(to, 128), :]
        for h in range(2):
            out[:, 512 + 128 * h : 640 + 128 * h] = total[512 + 128 * h : 640 + 128 * h, spot(to, 128)]


def place_back_kernel(co, total, *rest):
    pieces, (gate, up, down) = rest[:3], rest[3:6]
    zl = co[1]
    gate[:, spot(zl, 256)] = total[spot(zl, 128), 0:256]
    up[:, spot(zl, 256)] = total[spot(zl, 128), 256:512]
    down[spot(zl, 256), :] = total[512:768, spot(zl, 128)]
    for piece, off in zip(pieces, OFFS[1:]):
        at = lax.rem(zl - off + 4, 4)
        gate[:, spot(at, 256)] = piece[:, 0:256]
        up[:, spot(at, 256)] = piece[:, 256:512]
        for h in range(2):
            down[spot(at * 2 + h, 128), :] = piece[:, 512 + 128 * h : 640 + 128 * h]


def move(kernel, co, *args, out_shape):
    size = sum(a.size for a in args) * 2
    return pl.pallas_call(
        kernel,
        out_shape=out_shape,
        in_specs=[SMEM] + [VMEM] * len(args),
        out_specs=jax.tree.map(lambda _: VMEM, out_shape),
        cost_estimate=cost(0, size),
    )(co, *args)


def weight_copies(way, pieces, wide, down):
    gate_up, downs = [], []
    for x in range(4):
        for core in range(2):
            first = (x * 2 + core) * 768
            for part in range(2) if wide is not None else ():
                place = wide.at[pl.ds(x * 512, 512), pl.ds(512 * part + 256 * core, 256)]
                gate_up.append((pieces.at[pl.ds(first, 512), pl.ds(256 * part, 256)], place)[::way])
            if down is not None:
                place = down.at[pl.ds(256 * core, 256), pl.ds(x * 512, 512)]
                downs.append((pieces.at[pl.ds(first + 512, 256), :], place)[::way])
    return gate_up, downs


def whole_spot(y, z, whole):
    return whole.at[spot(lax.rem(z, 4), HALF), spot(y * 2 + z // 4, 256)]


def z_first_copies(co, way, pieces, whole):
    copies = []
    for n, off in enumerate(ZOFFS):
        at = lax.rem(co[5] - way * off + 8, 8)
        for o, y_off in enumerate(OFFS):
            piece = pieces[n] if n < 7 else pieces[7 + o // 2]
            src = piece.at[pl.ds((o if n < 7 else o % 2) * HALF, HALF), :]
            copies.append((src, whole_spot(lax.rem(co[2] - way * y_off + 4, 4), at, whole))[::way])
    return copies


def y_first_copies(co, way, pieces, whole):
    copies = []
    for k, piece in enumerate(pieces):
        y = lax.rem(co[2] - way * k * co[6] + 8, 4)
        for n, off in enumerate(ZOFFS):
            src = piece.at[pl.ds(n * HALF, HALF), :]
            copies.append((src, whole_spot(y, lax.rem(co[5] - way * off + 8, 8), whole))[::way])
    return copies


NN = (((1,), (0,)), ((), ()))
NT = (((1,), (1,)), ((), ()))


def dot(a, b, dims):
    return lax.dot_general(a, b, dims, preferred_element_type=F32)


def call(kernel, co, args, outs, scratch, sems, cost_estimate):
    return pl.pallas_call(
        kernel,
        out_shape=outs,
        in_specs=[SMEM] + [ANY] * len(args),
        out_specs=[ANY] * len(outs),
        scratch_shapes=[pltpu.VMEM(s, BF) for s in scratch] + [pltpu.SemaphoreType.DMA((sems,))],
        compiler_params=pltpu.CompilerParams(vmem_limit_bytes=VMEM_LIMIT),
        cost_estimate=cost_estimate,
    )(co, *args)


def layer_kernel(co, *refs):
    tok_in, cot_in, weights = refs[:9], refs[9:13], refs[13]
    mixed_out, back_out, terms_out = refs[14:23], refs[23:27], refs[27]
    tok, cot, wide, down, hid, grads, mixed, back, wide_grad, down_grad, limits, sems = refs[28:]
    zl, y, zh, c, z = co[1], co[2], co[3], co[4], co[5]
    scale = 1.0 / math.sqrt(TOK)
    gate_up, downs = weight_copies(1, weights, wide, down)
    limit_copies = []
    for n, off in enumerate(ZOFFS[:4]):
        at = lax.rem(z - off + 8, 4)
        limit_copies.append((tok_in[n].at[pl.ds(ROWS, 16), :], limits.at[spot(at, 16), :]))
    loads = gate_up + z_first_copies(co, 1, tok_in, tok) + limit_copies
    loads += y_first_copies(co, 1, cot_in, cot) + downs
    wait_all(run_copies(loads, sems))
    split = 128 - 64 * c

    @pl.loop(0, 2)
    def _(m):
        part = spot(m, 2 * HALF)
        pre = dot(tok[part, :], wide[...], NN)
        grad_hidden = dot(cot[part, :], down[...], NT)
        for core in range(2):
            first = ((y * 2 + zh) * 2 + core) * 1024 + zl * 256
            unit = (first + lax.broadcasted_iota(jnp.int32, (HALF, 256), 1)).astype(F32)
            row = lax.broadcasted_iota(jnp.int32, (HALF, 256), 0)
            for block in range(2):
                limit = limits[spot(2 * m + block, 16), :].astype(F32)
                keep = unit < jnp.where(row < split, limit[0:1], limit[1:2])
                near = slice(block * HALF, block * HALF + HALF)
                rows = spot(2 * m + block, HALF)
                g = pre[near, 256 * core : 256 * core + 256]
                u = pre[near, 512 + 256 * core : 768 + 256 * core]
                gh = grad_hidden[near, 256 * core : 256 * core + 256]
                sig = jax.nn.sigmoid(g)
                act = g * sig
                gate_part, up_part = pl.ds(256 * core, 256), pl.ds(512 + 256 * core, 256)
                hid[rows, gate_part] = jnp.where(keep, act * u, 0.0).astype(BF)
                grads[rows, gate_part] = jnp.where(
                    keep, gh * u * sig * (1.0 + g * (1.0 - sig)), 0.0
                ).astype(BF)
                grads[rows, up_part] = jnp.where(keep, gh * act, 0.0).astype(BF)

    @pl.loop(0, 2)
    def _(m):
        rows = spot(m, 384)
        mixed[rows, :] = dot(hid[rows, :], down[...], NN).astype(BF)

    kept = run_copies(z_first_copies(co, -1, mixed_out, mixed), sems, len(loads))

    @pl.loop(0, 2)
    def _(m):
        rows = spot(m, 384)
        back[rows, :] = dot(grads[rows, :], wide[...], NT).astype(BF)

    kept += run_copies(y_first_copies(co, -1, back_out, back), sems, len(loads) + len(kept))

    @pl.loop(0, 2)
    def _(n):
        block = spot(n, 1024)
        wide_grad[block, :] = (dot(tok[:, block].T, grads[...], NN) * scale).astype(BF)

    gate_up, downs = weight_copies(-1, terms_out, wide_grad, down_grad)
    kept += run_copies(gate_up, sems, len(loads) + len(kept))
    down_grad[...] = (dot(hid[...].T, cot[...], NN) * scale).astype(BF)
    kept += run_copies(downs, sems, len(loads) + len(kept))
    wait_all(kept)


def layer_call(co, tok_in, cot_in, weights):
    outs = [shape(ROWS, 256) for _ in range(7)] + [shape(ROWS // 2, 256) for _ in range(2)]
    outs += [shape(8 * HALF, 256) for _ in range(4)] + [shape(8 * 768, 512)]
    out = call(
        layer_kernel,
        co,
        (*tok_in, *cot_in, weights),
        outs,
        [(ROWS, D), (ROWS, D), (D, 2 * UNITS), (UNITS, D), (ROWS, UNITS), (ROWS, 2 * UNITS), (ROWS, D)]
        + [(ROWS, D), (D, 2 * UNITS), (UNITS, D), (64, 256)],
        92 + 32 + 32 + 24,
        cost(18 * ROWS * D * UNITS, 30e6),
    )
    return out[:9], out[9:13], out[13]


def add(*terms):
    total = terms[0].astype(F32)
    for term in terms[1:]:
        total = total + term.astype(F32)
    return total.astype(BF)


def by_core(c, kept, got, axis):
    return jnp.where(c == 0, jnp.concatenate([kept, got], axis), jnp.concatenate([got, kept], axis))


def pick(value, at, size, axis):
    return lax.dynamic_slice_in_dim(value, at * size, size, axis)


def local(tokens, cotangent, prefix, gate_weight, up_weight, down_weight):
    x, zl, y, zh, c = (lax.axis_index(a) for a in ("x", "zl", "y", "zh", "c"))
    co = jnp.stack([x, zl, y, zh, c, zh * 4 + zl, 1 - 2 * c, x]).astype(jnp.int32)

    w = list(move(pack_kernel, co, gate_weight, up_weight, down_weight, out_shape=[shape(128, 768)] * 3))
    away = swap(jnp.concatenate([pick(tokens, 1 - c, HALF, 0), pick(cotangent, 1 - c, HALF, 0)]))
    tok = by_core(c, pick(tokens, c, HALF, 0), away[:HALF], 1)
    cot = by_core(c, pick(cotangent, c, HALF, 0), away[HALF:], 1)
    mine = lax.dynamic_slice_in_dim(prefix, c, 2).astype(BF)
    limits = jnp.broadcast_to(jnp.pad(mine, (0, 14))[:, None], (16, 256))

    got0, got1 = shift(w[0], "zl", OFFS[1]), shift(w[1], "zl", OFFS[2])
    tok_y = [shift(tok, "y", off) for off in OFFS[1:]]
    *tok_y, cot, got0, got1, w[2] = together(*tok_y, cot, got0, got1, w[2])
    up1, down1, got2 = shift_z(cot, 1), shift_z(cot, -1), shift(w[2], "zl", OFFS[3])
    up2, down2 = shift_z(up1, 1), shift_z(down1, -1)
    up3, down3 = shift_z(up2, 1), shift_z(down2, -1)
    up3, down3, got2 = together(up3, down3, got2)
    up4, down4 = shift_z(up3[: HALF // 2], 1), shift_z(down3[HALF // 2 :], -1)
    placed = move(
        place_kernel, co, gate_weight, up_weight, down_weight, got0, got1, got2, out_shape=shape(768, 512)
    )
    weights = lax.all_gather(placed, ("x", "c"), axis=0, tiled=True)
    up4, down4, *tok_y = together(up4, down4, *tok_y)
    cot_in = [jnp.concatenate([cot, up1, down1, up2, down2, up3, down3, up4, down4])]
    tok_in = [jnp.concatenate([tok, *tok_y, limits])]
    up = down = tok_in[0]
    for _ in range(3):
        got_y, up, down = spin(cot_in[-1], "y"), shift_z(up, 1), shift_z(down, -1)
        got_y, up, down = together(got_y, up, down)
        tok_in += [up, down]
        cot_in.append(got_y)
    tok_in += [shift_z(up[: ROWS // 2], 1), shift_z(down[ROWS // 2 : ROWS], -1)]

    mixed_terms, back_terms, terms = layer_call(co, tok_in, cot_in, weights)
    total = lax.psum_scatter(terms, ("x", "c"), scatter_dimension=0, tiled=True)

    back, up, down = spin(back_terms[3], "y"), shift_z(mixed_terms[7], 1), shift_z(mixed_terms[8], -1)
    back, up, down = together(back, up, down)
    half = ROWS // 2
    up = jnp.concatenate([add(mixed_terms[5][:half], up), mixed_terms[5][half:]])
    down = jnp.concatenate([mixed_terms[6][:half], add(mixed_terms[6][half:], down)])
    back = add(back_terms[2], back)
    for k in (2, 1):
        back, up, down = spin(back, "y"), shift_z(up, 1), shift_z(down, -1)
        back, up, down = together(back, up, down)
        up, down = add(mixed_terms[2 * k - 1], up), add(mixed_terms[2 * k], down)
        back = add(back_terms[k - 1], back)
    pieces = [back[n * HALF : (n + 1) * HALF] for n in range(8)]

    up, down, near_up, near_down = shift_z(up, 1), shift_z(down, -1), shift_z(pieces[1], 1), shift_z(pieces[2], -1)
    up, down, near_up, near_down, co = together(up, down, near_up, near_down, co)
    mixed = add(mixed_terms[0], up, down)
    w = list(move(pack_back_kernel, co, total, out_shape=[shape(128, 768)] * 3))

    half = HALF // 2
    up, down = shift_z(pieces[5], 1), shift_z(pieces[6], -1)
    far_up, far_down = shift_z(pieces[7][:half], 2), shift_z(pieces[7][half:], -2)
    got0 = shift(w[0], "zl", OFFS[1])
    up, down, far_up, far_down, got0, w[1], w[2] = together(up, down, far_up, far_down, got0, w[1], w[2])
    up = jnp.concatenate([add(pieces[3][:half], up[:half], far_up), add(pieces[3][half:], up[half:])])
    down = jnp.concatenate([add(pieces[4][:half], down[:half]), add(pieces[4][half:], down[half:], far_down)])

    up, down, got1 = shift_z(up, 2), shift_z(down, -2), shift(w[1], "zl", OFFS[2])
    mixed_y = [shift(mixed[o * HALF : (o + 1) * HALF], "y", OFFS[o]) for o in range(1, 3)]
    up, down, got1, w[2], mixed, *mixed_y = together(up, down, got1, w[2], mixed, *mixed_y)
    back = add(pieces[0], near_up, near_down, up, down)

    got2 = shift(w[2], "zl", OFFS[3])
    mixed = add(mixed[:HALF], *mixed_y, shift(mixed[3 * HALF :], "y", OFFS[3]))
    away = swap(jnp.concatenate([pick(mixed, 1 - c, 128, 1), pick(back, 1 - c, 128, 1)]))
    mixed = by_core(c, pick(mixed, c, 128, 1), away[:HALF], 0)
    input_grad = by_core(c, pick(back, c, 128, 1), away[HALF:], 0)
    gate_grad, up_grad, down_grad = move(
        place_back_kernel,
        co,
        total,
        got0,
        got1,
        got2,
        out_shape=[shape(128, 1024), shape(128, 1024), shape(1024, 128)],
    )
    return mixed, input_grad, gate_grad, up_grad, down_grad


def solution(mesh):
    fine = Mesh(mesh.devices.reshape(4, 4, 4, 2, 2), ("x", "zl", "y", "zh", "c"))
    rows, columns = ("x", "zl"), ("y", "zh", "c")
    return jax.shard_map(
        local,
        mesh=fine,
        in_specs=(
            P(rows, columns),
            P(rows, columns),
            P(rows),
            P(rows, columns),
            P(rows, columns),
            P(columns, rows),
        ),
        out_specs=(
            P(rows, columns),
            P(rows, columns),
            P(rows, columns),
            P(rows, columns),
            P(columns, rows),
        ),
        check_vma=False,
    )
```

```python
import math

import jax
import jax.numpy as jnp
from jax import lax
from jax.experimental import pallas as pl
from jax.experimental.pallas import tpu as pltpu
from jax.sharding import Mesh
from jax.sharding import PartitionSpec as P


D = 2048
TOK = 6144
BF = jnp.bfloat16
F32 = jnp.float32
HALF = 192
ROWS = 768
UNITS = 512
OFFS = (0, 1, -1, 2)
ZOFFS = (0, 1, -1, 2, -2, 3, -3, 4)
VMEM_LIMIT = 58 * 1024 * 1024
ANY = pl.BlockSpec(memory_space=pl.ANY)
VMEM = pl.BlockSpec(memory_space=pltpu.VMEM)
SMEM = pl.BlockSpec(memory_space=pltpu.SMEM)


def shift(value, axis, by):
    return lax.ppermute(value, axis, [(i, (i + by) % 4) for i in range(4)])


def shift_z(value, by):
    pairs = []
    for z in range(8):
        to = (z + by) % 8
        pairs.append(((z % 4) * 2 + z // 4, (to % 4) * 2 + to // 4))
    return lax.ppermute(value, ("zl", "zh"), pairs)


def spin(value, axis):
    pairs = [(2 * i + c, (i + (1, -1)[c]) % 4 * 2 + c) for i in range(4) for c in range(2)]
    return lax.ppermute(value, (axis, "c"), pairs)


def together(*values):
    return lax.optimization_barrier(values)


def swap(value):
    return lax.ppermute(value, "c", [(0, 1), (1, 0)])


def run_copies(copies, sems, first=0):
    started = []
    for n, (src, dst) in enumerate(copies):
        copy = pltpu.make_async_copy(src, dst, sems.at[first + n])
        copy.start()
        started.append(copy)
    return started


def wait_all(started):
    for copy in started:
        copy.wait()


def spot(value, step):
    return pl.ds(pl.multiple_of(value * step, step), step)


def cost(flops, size):
    return pl.CostEstimate(flops=int(flops), bytes_accessed=int(size), transcendentals=0)


def shape(*dims):
    return jax.ShapeDtypeStruct(dims, BF)


def pack_kernel(co, gate, up, down, *outs):
    zl = co[1]
    for out, off in zip(outs, OFFS[1:]):
        to = lax.rem(zl + off + 4, 4)
        out[:, 0:256] = gate[:, spot(to, 256)]
        out[:, 256:512] = up[:, spot(to, 256)]
        for h in range(2):
            out[:, 512 + 128 * h : 640 + 128 * h] = down[spot(to * 2 + h, 128), :]


def place_kernel(co, gate, up, down, *rest):
    pieces, out = rest[:3], rest[3]
    zl = co[1]
    out[spot(zl, 128), 0:256] = gate[:, spot(zl, 256)]
    out[spot(zl, 128), 256:512] = up[:, spot(zl, 256)]
    out[512:768, spot(zl, 128)] = down[spot(zl, 256), :]
    for piece, off in zip(pieces, OFFS[1:]):
        at = lax.rem(zl - off + 4, 4)
        out[spot(at, 128), :] = piece[:, 0:512]
        for h in range(2):
            out[512 + 128 * h : 640 + 128 * h, spot(at, 128)] = piece[:, 512 + 128 * h : 640 + 128 * h]


def pack_back_kernel(co, total, *outs):
    zl = co[1]
    for out, off in zip(outs, OFFS[1:]):
        to = lax.rem(zl + off + 4, 4)
        out[:, 0:512] = total[spot(to, 128), :]
        for h in range(2):
            out[:, 512 + 128 * h : 640 + 128 * h] = total[512 + 128 * h : 640 + 128 * h, spot(to, 128)]


def place_back_kernel(co, total, *rest):
    pieces, (gate, up, down) = rest[:3], rest[3:6]
    zl = co[1]
    gate[:, spot(zl, 256)] = total[spot(zl, 128), 0:256]
    up[:, spot(zl, 256)] = total[spot(zl, 128), 256:512]
    down[spot(zl, 256), :] = total[512:768, spot(zl, 128)]
    for piece, off in zip(pieces, OFFS[1:]):
        at = lax.rem(zl - off + 4, 4)
        gate[:, spot(at, 256)] = piece[:, 0:256]
        up[:, spot(at, 256)] = piece[:, 256:512]
        for h in range(2):
            down[spot(at * 2 + h, 128), :] = piece[:, 512 + 128 * h : 640 + 128 * h]


def move(kernel, co, *args, out_shape):
    size = sum(a.size for a in args) * 2
    return pl.pallas_call(
        kernel,
        out_shape=out_shape,
        in_specs=[SMEM] + [VMEM] * len(args),
        out_specs=jax.tree.map(lambda _: VMEM, out_shape),
        cost_estimate=cost(0, size),
    )(co, *args)


def weight_copies(way, pieces, wide, down):
    gate_up, downs = [], []
    for x in range(4):
        for core in range(2):
            first = (x * 2 + core) * 768
            for part in range(2) if wide is not None else ():
                place = wide.at[pl.ds(x * 512, 512), pl.ds(512 * part + 256 * core, 256)]
                gate_up.append((pieces.at[pl.ds(first, 512), pl.ds(256 * part, 256)], place)[::way])
            if down is not None:
                place = down.at[pl.ds(256 * core, 256), pl.ds(x * 512, 512)]
                downs.append((pieces.at[pl.ds(first + 512, 256), :], place)[::way])
    return gate_up, downs


def whole_spot(y, z, whole):
    return whole.at[spot(lax.rem(z, 4), HALF), spot(y * 2 + z // 4, 256)]


def z_first_copies(co, way, pieces, whole):
    copies = []
    for n, off in enumerate(ZOFFS):
        at = lax.rem(co[5] - way * off + 8, 8)
        for o, y_off in enumerate(OFFS):
            piece = pieces[n] if n < 7 else pieces[7 + o // 2]
            src = piece.at[pl.ds((o if n < 7 else o % 2) * HALF, HALF), :]
            copies.append((src, whole_spot(lax.rem(co[2] - way * y_off + 4, 4), at, whole))[::way])
    return copies


def y_first_copies(co, way, pieces, whole):
    copies = []
    for k in range(4):
        y = lax.rem(co[2] - way * k * co[6] + 8, 4)
        for n, off in enumerate(ZOFFS):
            src = pieces[2 * k + n // 4].at[pl.ds(n % 4 * HALF, HALF), :]
            copies.append((src, whole_spot(y, lax.rem(co[5] - way * off + 8, 8), whole))[::way])
    return copies


NN = (((1,), (0,)), ((), ()))
NT = (((1,), (1,)), ((), ()))


def dot(a, b, dims):
    return lax.dot_general(a, b, dims, preferred_element_type=F32)


def call(kernel, co, args, outs, scratch, sems, cost_estimate):
    return pl.pallas_call(
        kernel,
        out_shape=outs,
        in_specs=[SMEM] + [ANY] * len(args),
        out_specs=[ANY] * len(outs),
        scratch_shapes=[pltpu.VMEM(s, BF) for s in scratch] + [pltpu.SemaphoreType.DMA((sems,))],
        compiler_params=pltpu.CompilerParams(vmem_limit_bytes=VMEM_LIMIT),
        cost_estimate=cost_estimate,
    )(co, *args)


def layer_kernel(co, *refs):
    tok_in, cot_in, weights = refs[:9], refs[9:17], refs[17]
    mixed_out, back_out, terms_out = refs[18:27], refs[27:35], refs[35]
    tok, cot, wide, down, hid, grads, mixed, back, wide_grad, down_grad, limits, sems = refs[36:]
    zl, y, zh, c, z = co[1], co[2], co[3], co[4], co[5]
    scale = 1.0 / math.sqrt(TOK)
    gate_up, downs = weight_copies(1, weights, wide, down)
    limit_copies = []
    for n, off in enumerate(ZOFFS[:4]):
        at = lax.rem(z - off + 8, 4)
        limit_copies.append((tok_in[n].at[pl.ds(ROWS, 16), :], limits.at[spot(at, 16), :]))
    loads = gate_up + z_first_copies(co, 1, tok_in, tok) + limit_copies
    early = run_copies(loads, sems)
    late = run_copies(y_first_copies(co, 1, cot_in, cot) + downs, sems, len(early))
    used = len(early) + len(late)
    wait_all(early)
    split = 128 - 64 * c

    for m in range(2):
        part = pl.ds(m * 2 * HALF, 2 * HALF)
        pre = dot(tok[part, :], wide[...], NN)
        if m == 0:
            wait_all(late)
        grad_hidden = dot(cot[part, :], down[...], NT)
        for core in range(2):
            first = ((y * 2 + zh) * 2 + core) * 1024 + zl * 256
            unit = (first + lax.broadcasted_iota(jnp.int32, (HALF, 256), 1)).astype(F32)
            row = lax.broadcasted_iota(jnp.int32, (HALF, 256), 0)
            for block in range(2):
                limit = limits[pl.ds(16 * (2 * m + block), 16), :].astype(F32)
                keep = unit < jnp.where(row < split, limit[0:1], limit[1:2])
                near = slice(block * HALF, block * HALF + HALF)
                rows = pl.ds((2 * m + block) * HALF, HALF)
                g = pre[near, 256 * core : 256 * core + 256]
                u = pre[near, 512 + 256 * core : 768 + 256 * core]
                gh = grad_hidden[near, 256 * core : 256 * core + 256]
                sig = jax.nn.sigmoid(g)
                act = g * sig
                gate_part, up_part = pl.ds(256 * core, 256), pl.ds(512 + 256 * core, 256)
                hid[rows, gate_part] = jnp.where(keep, act * u, 0.0).astype(BF)
                grads[rows, gate_part] = jnp.where(
                    keep, gh * u * sig * (1.0 + g * (1.0 - sig)), 0.0
                ).astype(BF)
                grads[rows, up_part] = jnp.where(keep, gh * act, 0.0).astype(BF)

    @pl.loop(0, 2)
    def _(m):
        rows = spot(m, 384)
        mixed[rows, :] = dot(hid[rows, :], down[...], NN).astype(BF)

    kept = run_copies(z_first_copies(co, -1, mixed_out, mixed), sems, used)

    @pl.loop(0, 2)
    def _(m):
        rows = spot(m, 384)
        back[rows, :] = dot(grads[rows, :], wide[...], NT).astype(BF)

    kept += run_copies(y_first_copies(co, -1, back_out, back), sems, used + len(kept))

    @pl.loop(0, 2)
    def _(n):
        block = spot(n, 1024)
        wide_grad[block, :] = (dot(tok[:, block].T, grads[...], NN) * scale).astype(BF)

    gate_up, downs = weight_copies(-1, terms_out, wide_grad, down_grad)
    kept += run_copies(gate_up, sems, used + len(kept))
    down_grad[...] = (dot(hid[...].T, cot[...], NN) * scale).astype(BF)
    kept += run_copies(downs, sems, used + len(kept))
    wait_all(kept)


def layer_call(co, tok_in, cot_in, weights):
    outs = [shape(ROWS, 256) for _ in range(7)] + [shape(ROWS // 2, 256) for _ in range(2)]
    outs += [shape(4 * HALF, 256) for _ in range(8)] + [shape(8 * 768, 512)]
    out = call(
        layer_kernel,
        co,
        (*tok_in, *cot_in, weights),
        outs,
        [(ROWS, D), (ROWS, D), (D, 2 * UNITS), (UNITS, D), (ROWS, UNITS), (ROWS, 2 * UNITS), (ROWS, D)]
        + [(ROWS, D), (D, 2 * UNITS), (UNITS, D), (64, 256)],
        92 + 32 + 32 + 24,
        cost(18 * ROWS * D * UNITS, 30e6),
    )
    return out[:9], out[9:17], out[17]


def add(*terms):
    total = terms[0].astype(F32)
    for term in terms[1:]:
        total = total + term.astype(F32)
    return total.astype(BF)


def by_core(c, kept, got, axis):
    return jnp.where(c == 0, jnp.concatenate([kept, got], axis), jnp.concatenate([got, kept], axis))


def pick(value, at, size, axis):
    return lax.dynamic_slice_in_dim(value, at * size, size, axis)


def local(tokens, cotangent, prefix, gate_weight, up_weight, down_weight):
    x, zl, y, zh, c = (lax.axis_index(a) for a in ("x", "zl", "y", "zh", "c"))
    co = jnp.stack([x, zl, y, zh, c, zh * 4 + zl, 1 - 2 * c, x]).astype(jnp.int32)

    w = list(move(pack_kernel, co, gate_weight, up_weight, down_weight, out_shape=[shape(128, 768)] * 3))
    tokens, cotangent, *w = together(tokens, cotangent, *w)
    away = swap(jnp.concatenate([pick(tokens, 1 - c, HALF, 0), pick(cotangent, 1 - c, HALF, 0)]))
    tok = by_core(c, pick(tokens, c, HALF, 0), away[:HALF], 1)
    cot = by_core(c, pick(cotangent, c, HALF, 0), away[HALF:], 1)
    mine = lax.dynamic_slice_in_dim(prefix, c, 2).astype(BF)
    limits = jnp.broadcast_to(jnp.pad(mine, (0, 14))[:, None], (16, 256))

    got0, got1, got2 = (shift(v, "zl", off) for v, off in zip(w, OFFS[1:]))
    tok_y = [shift(tok, "y", off) for off in OFFS[1:]]
    *tok_y, cot, got0, got1 = together(*tok_y, cot, got0, got1)
    up1, down1, up2, down2 = shift_z(cot, 1), shift_z(cot, -1), shift_z(cot, 2), shift_z(cot, -2)
    up1, down1, up2, down2, got2 = together(up1, down1, up2, down2, got2)
    placed = move(
        place_kernel, co, gate_weight, up_weight, down_weight, got0, got1, got2, out_shape=shape(768, 512)
    )
    weights = lax.all_gather(placed, ("x", "c"), axis=0, tiled=True)
    half = HALF // 2
    up3, down3, up4, down4 = together(
        shift_z(up2, 1), shift_z(down2, -1), shift_z(up2[:half], 2), shift_z(down2[half:], -2)
    )
    cot_in = [jnp.concatenate([cot, up1, down1, up2]), jnp.concatenate([down2, up3, down3, up4, down4])]
    tok_in = [jnp.concatenate([tok, *tok_y, limits])]
    up = down = tok_in[0]
    for _ in range(3):
        up, down = shift_z(up, 1), shift_z(down, -1)
        tok_in += [up, down]
    for _ in range(3):
        cot_in += [spin(cot_in[-2], "y"), spin(cot_in[-1], "y")]
    tok_in += [shift_z(up[: ROWS // 2], 1), shift_z(down[ROWS // 2 : ROWS], -1)]

    mixed_terms, back_terms, terms = layer_call(co, tok_in, cot_in, weights)
    total = lax.psum_scatter(terms, ("x", "c"), scatter_dimension=0, tiled=True)

    up, down = shift_z(mixed_terms[7], 1), shift_z(mixed_terms[8], -1)
    half = ROWS // 2
    up = jnp.concatenate([add(mixed_terms[5][:half], up), mixed_terms[5][half:]])
    down = jnp.concatenate([mixed_terms[6][:half], add(mixed_terms[6][half:], down)])
    outer, inner = back_terms[7], back_terms[6]
    for k in (2, 1, 0):
        outer, inner = add(back_terms[2 * k + 1], spin(outer, "y")), add(back_terms[2 * k], spin(inner, "y"))
        if k > 0:
            up, down = shift_z(up, 1), shift_z(down, -1)
            up, down = add(mixed_terms[2 * k - 1], up), add(mixed_terms[2 * k], down)
    pieces = [v[n * HALF : (n + 1) * HALF] for v in (inner, outer) for n in range(4)]

    half = HALF // 2
    far_up, far_down = shift_z(pieces[7][:half], 2), shift_z(pieces[7][half:], -2)
    third_up, third_down = shift_z(pieces[5], 1), shift_z(pieces[6], -1)
    up, down = shift_z(up, 1), shift_z(down, -1)
    up, down, far_up, far_down, third_up, third_down = together(
        up, down, far_up, far_down, third_up, third_down
    )
    mixed = add(mixed_terms[0], up, down)
    up = jnp.concatenate([add(pieces[3][:half], third_up[:half], far_up), add(pieces[3][half:], third_up[half:])])
    down = jnp.concatenate(
        [add(pieces[4][:half], third_down[:half]), add(pieces[4][half:], third_down[half:], far_down)]
    )
    near_up, near_down, up, down = shift_z(pieces[1], 1), shift_z(pieces[2], -1), shift_z(up, 2), shift_z(down, -2)
    mixed_y = [shift(mixed[o * HALF : (o + 1) * HALF], "y", OFFS[o]) for o in range(1, 4)]
    near_up, near_down, mixed_y[0], co = together(near_up, near_down, mixed_y[0], co)
    back = add(pieces[0], near_up, near_down, up, down)
    mixed = add(mixed[:HALF], *mixed_y)
    w = move(pack_back_kernel, co, total, out_shape=[shape(128, 768)] * 3)
    got = [shift(v, "zl", off) for v, off in zip(w, OFFS[1:])]
    mixed, back, got[0] = together(mixed, back, got[0])
    away = swap(jnp.concatenate([pick(mixed, 1 - c, 128, 1), pick(back, 1 - c, 128, 1)]))
    mixed = by_core(c, pick(mixed, c, 128, 1), away[:HALF], 0)
    input_grad = by_core(c, pick(back, c, 128, 1), away[HALF:], 0)
    gate_grad, up_grad, down_grad = move(
        place_back_kernel,
        co,
        total,
        *got,
        out_shape=[shape(128, 1024), shape(128, 1024), shape(1024, 128)],
    )
    return mixed, input_grad, gate_grad, up_grad, down_grad


def solution(mesh):
    fine = Mesh(mesh.devices.reshape(4, 4, 4, 2, 2), ("x", "zl", "y", "zh", "c"))
    rows, columns = ("x", "zl"), ("y", "zh", "c")
    return jax.shard_map(
        local,
        mesh=fine,
        in_specs=(
            P(rows, columns),
            P(rows, columns),
            P(rows),
            P(rows, columns),
            P(rows, columns),
            P(columns, rows),
        ),
        out_specs=(
            P(rows, columns),
            P(rows, columns),
            P(rows, columns),
            P(rows, columns),
            P(columns, rows),
        ),
        check_vma=False,
    )
```

```python
import math

import jax
import jax.numpy as jnp
from jax import lax
from jax.experimental import pallas as pl
from jax.experimental.pallas import tpu as pltpu
from jax.sharding import Mesh
from jax.sharding import PartitionSpec as P


D = 2048
TOK = 6144
BF = jnp.bfloat16
F32 = jnp.float32
HALF = 192
ROWS = 768
UNITS = 512
OFFS = (0, 1, -1, 2)
ZOFFS = (0, 1, -1, 2, -2, 3, -3, 4)
VMEM_LIMIT = 58 * 1024 * 1024
ANY = pl.BlockSpec(memory_space=pl.ANY)
VMEM = pl.BlockSpec(memory_space=pltpu.VMEM)
SMEM = pl.BlockSpec(memory_space=pltpu.SMEM)


def shift(value, axis, by):
    return lax.ppermute(value, axis, [(i, (i + by) % 4) for i in range(4)])


def shift_z(value, by):
    pairs = []
    for z in range(8):
        to = (z + by) % 8
        pairs.append(((z % 4) * 2 + z // 4, (to % 4) * 2 + to // 4))
    return lax.ppermute(value, ("zl", "zh"), pairs)


def together(*values):
    return lax.optimization_barrier(values)


def swap(value):
    return lax.ppermute(value, "c", [(0, 1), (1, 0)])


def run_copies(copies, sems, first=0):
    started = []
    for n, (src, dst) in enumerate(copies):
        copy = pltpu.make_async_copy(src, dst, sems.at[first + n])
        copy.start()
        started.append(copy)
    return started


def wait_all(started):
    for copy in started:
        copy.wait()


def spot(value, step):
    return pl.ds(pl.multiple_of(value * step, step), step)


def cost(flops, size):
    return pl.CostEstimate(flops=int(flops), bytes_accessed=int(size), transcendentals=0)


def shape(*dims):
    return jax.ShapeDtypeStruct(dims, BF)


def pack_kernel(co, gate, up, down, *outs):
    zl = co[1]
    for out, off in zip(outs, OFFS[1:]):
        to = lax.rem(zl + off + 4, 4)
        out[:, 0:256] = gate[:, spot(to, 256)]
        out[:, 256:512] = up[:, spot(to, 256)]
        for h in range(2):
            out[:, 512 + 128 * h : 640 + 128 * h] = down[spot(to * 2 + h, 128), :]


def place_kernel(co, gate, up, down, *rest):
    pieces, out = rest[:3], rest[3]
    zl = co[1]
    out[spot(zl, 128), 0:256] = gate[:, spot(zl, 256)]
    out[spot(zl, 128), 256:512] = up[:, spot(zl, 256)]
    out[512:768, spot(zl, 128)] = down[spot(zl, 256), :]
    for piece, off in zip(pieces, OFFS[1:]):
        at = lax.rem(zl - off + 4, 4)
        out[spot(at, 128), :] = piece[:, 0:512]
        for h in range(2):
            out[512 + 128 * h : 640 + 128 * h, spot(at, 128)] = piece[:, 512 + 128 * h : 640 + 128 * h]


def pack_back_kernel(co, total, *outs):
    zl = co[1]
    for out, off in zip(outs, OFFS[1:]):
        to = lax.rem(zl + off + 4, 4)
        out[:, 0:512] = total[spot(to, 128), :]
        for h in range(2):
            out[:, 512 + 128 * h : 640 + 128 * h] = total[512 + 128 * h : 640 + 128 * h, spot(to, 128)]


def place_back_kernel(co, total, *rest):
    pieces, (gate, up, down) = rest[:3], rest[3:6]
    zl = co[1]
    gate[:, spot(zl, 256)] = total[spot(zl, 128), 0:256]
    up[:, spot(zl, 256)] = total[spot(zl, 128), 256:512]
    down[spot(zl, 256), :] = total[512:768, spot(zl, 128)]
    for piece, off in zip(pieces, OFFS[1:]):
        at = lax.rem(zl - off + 4, 4)
        gate[:, spot(at, 256)] = piece[:, 0:256]
        up[:, spot(at, 256)] = piece[:, 256:512]
        for h in range(2):
            down[spot(at * 2 + h, 128), :] = piece[:, 512 + 128 * h : 640 + 128 * h]


def move(kernel, co, *args, out_shape):
    size = sum(a.size for a in args) * 2
    return pl.pallas_call(
        kernel,
        out_shape=out_shape,
        in_specs=[SMEM] + [VMEM] * len(args),
        out_specs=jax.tree.map(lambda _: VMEM, out_shape),
        cost_estimate=cost(0, size),
    )(co, *args)


def weight_copies(way, pieces, wide, down):
    gate_up, downs = [], []
    for x in range(4):
        for core in range(2):
            first = (x * 2 + core) * 768
            for part in range(2) if wide is not None else ():
                place = wide.at[pl.ds(x * 512, 512), pl.ds(512 * part + 256 * core, 256)]
                gate_up.append((pieces.at[pl.ds(first, 512), pl.ds(256 * part, 256)], place)[::way])
            if down is not None:
                place = down.at[pl.ds(256 * core, 256), pl.ds(x * 512, 512)]
                downs.append((pieces.at[pl.ds(first + 512, 256), :], place)[::way])
    return gate_up, downs


def whole_spot(y, z, whole):
    return whole.at[spot(lax.rem(z, 4), HALF), spot(y * 2 + z // 4, 256)]


def z_first_copies(co, way, pieces, whole):
    copies = []
    for n, off in enumerate(ZOFFS):
        at = lax.rem(co[5] - way * off + 8, 8)
        for o, y_off in enumerate(OFFS):
            piece = pieces[n] if n < 7 else pieces[7 + o // 2]
            src = piece.at[pl.ds((o if n < 7 else o % 2) * HALF, HALF), :]
            copies.append((src, whole_spot(lax.rem(co[2] - way * y_off + 4, 4), at, whole))[::way])
    return copies


def y_first_copies(co, way, pieces, whole):
    copies = []
    for k in range(4):
        for n, off in enumerate(ZOFFS):
            y = lax.rem(co[2] - way * k * (1 if n < 4 else -1) + 8, 4)
            src = pieces[2 * k + n // 4].at[pl.ds(n % 4 * HALF, HALF), :]
            copies.append((src, whole_spot(y, lax.rem(co[5] - way * off + 8, 8), whole))[::way])
    return copies


NN = (((1,), (0,)), ((), ()))
NT = (((1,), (1,)), ((), ()))


def dot(a, b, dims):
    return lax.dot_general(a, b, dims, preferred_element_type=F32)


def call(kernel, co, args, outs, scratch, sems, cost_estimate):
    return pl.pallas_call(
        kernel,
        out_shape=outs,
        in_specs=[SMEM] + [ANY] * len(args),
        out_specs=[ANY] * len(outs),
        scratch_shapes=[pltpu.VMEM(s, BF) for s in scratch] + [pltpu.SemaphoreType.DMA((sems,))],
        compiler_params=pltpu.CompilerParams(vmem_limit_bytes=VMEM_LIMIT),
        cost_estimate=cost_estimate,
    )(co, *args)


def layer_kernel(co, *refs):
    tok_in, cot_in, weights = refs[:9], refs[9:17], refs[17]
    mixed_out, back_out, terms_out = refs[18:27], refs[27:35], refs[35]
    tok, cot, wide, down, hid, grads, mixed, back, wide_grad, down_grad, limits, sems = refs[36:]
    zl, y, zh, c, z = co[1], co[2], co[3], co[4], co[5]
    scale = 1.0 / math.sqrt(TOK)
    gate_up, downs = weight_copies(1, weights, wide, down)
    limit_copies = []
    for n, off in enumerate(ZOFFS[:4]):
        at = lax.rem(z - off + 8, 4)
        limit_copies.append((tok_in[n].at[pl.ds(ROWS, 16), :], limits.at[spot(at, 16), :]))
    loads = gate_up + z_first_copies(co, 1, tok_in, tok) + limit_copies
    early = run_copies(loads, sems)
    late = run_copies(y_first_copies(co, 1, cot_in, cot) + downs, sems, len(early))
    used = len(early) + len(late)
    wait_all(early)
    split = 128 - 64 * c

    for m in range(2):
        part = pl.ds(m * 2 * HALF, 2 * HALF)
        pre = dot(tok[part, :], wide[...], NN)
        if m == 0:
            wait_all(late)
        grad_hidden = dot(cot[part, :], down[...], NT)
        for core in range(2):
            first = ((y * 2 + zh) * 2 + core) * 1024 + zl * 256
            unit = (first + lax.broadcasted_iota(jnp.int32, (HALF, 256), 1)).astype(F32)
            row = lax.broadcasted_iota(jnp.int32, (HALF, 256), 0)
            for block in range(2):
                limit = limits[pl.ds(16 * (2 * m + block), 16), :].astype(F32)
                keep = unit < jnp.where(row < split, limit[0:1], limit[1:2])
                near = slice(block * HALF, block * HALF + HALF)
                rows = pl.ds((2 * m + block) * HALF, HALF)
                g = pre[near, 256 * core : 256 * core + 256]
                u = pre[near, 512 + 256 * core : 768 + 256 * core]
                gh = grad_hidden[near, 256 * core : 256 * core + 256]
                sig = jax.nn.sigmoid(g)
                act = g * sig
                gate_part, up_part = pl.ds(256 * core, 256), pl.ds(512 + 256 * core, 256)
                hid[rows, gate_part] = jnp.where(keep, act * u, 0.0).astype(BF)
                grads[rows, gate_part] = jnp.where(
                    keep, gh * u * sig * (1.0 + g * (1.0 - sig)), 0.0
                ).astype(BF)
                grads[rows, up_part] = jnp.where(keep, gh * act, 0.0).astype(BF)

    @pl.loop(0, 2)
    def _(m):
        rows = spot(m, 384)
        mixed[rows, :] = dot(hid[rows, :], down[...], NN).astype(BF)

    kept = run_copies(z_first_copies(co, -1, mixed_out, mixed), sems, used)

    @pl.loop(0, 2)
    def _(m):
        rows = spot(m, 384)
        back[rows, :] = dot(grads[rows, :], wide[...], NT).astype(BF)

    kept += run_copies(y_first_copies(co, -1, back_out, back), sems, used + len(kept))

    @pl.loop(0, 2)
    def _(n):
        block = spot(n, 1024)
        wide_grad[block, :] = (dot(tok[:, block].T, grads[...], NN) * scale).astype(BF)

    gate_up, downs = weight_copies(-1, terms_out, wide_grad, down_grad)
    kept += run_copies(gate_up, sems, used + len(kept))
    down_grad[...] = (dot(hid[...].T, cot[...], NN) * scale).astype(BF)
    kept += run_copies(downs, sems, used + len(kept))
    wait_all(kept)


def layer_call(co, tok_in, cot_in, weights):
    outs = [shape(ROWS, 256) for _ in range(7)] + [shape(ROWS // 2, 256) for _ in range(2)]
    outs += [shape(4 * HALF, 256) for _ in range(8)] + [shape(8 * 768, 512)]
    out = call(
        layer_kernel,
        co,
        (*tok_in, *cot_in, weights),
        outs,
        [(ROWS, D), (ROWS, D), (D, 2 * UNITS), (UNITS, D), (ROWS, UNITS), (ROWS, 2 * UNITS), (ROWS, D)]
        + [(ROWS, D), (D, 2 * UNITS), (UNITS, D), (64, 256)],
        92 + 32 + 32 + 24,
        cost(18 * ROWS * D * UNITS, 30e6),
    )
    return out[:9], out[9:17], out[17]


def add(*terms):
    total = terms[0].astype(F32)
    for term in terms[1:]:
        total = total + term.astype(F32)
    return total.astype(BF)


def by_core(c, kept, got, axis):
    return jnp.where(c == 0, jnp.concatenate([kept, got], axis), jnp.concatenate([got, kept], axis))


def pick(value, at, size, axis):
    return lax.dynamic_slice_in_dim(value, at * size, size, axis)


def local(tokens, cotangent, prefix, gate_weight, up_weight, down_weight):
    x, zl, y, zh, c = (lax.axis_index(a) for a in ("x", "zl", "y", "zh", "c"))
    co = jnp.stack([x, zl, y, zh, c, zh * 4 + zl]).astype(jnp.int32)

    w = list(move(pack_kernel, co, gate_weight, up_weight, down_weight, out_shape=[shape(128, 768)] * 3))
    tokens, cotangent, *w = together(tokens, cotangent, *w)
    away = swap(jnp.concatenate([pick(tokens, 1 - c, HALF, 0), pick(cotangent, 1 - c, HALF, 0)]))
    tok = by_core(c, pick(tokens, c, HALF, 0), away[:HALF], 1)
    cot = by_core(c, pick(cotangent, c, HALF, 0), away[HALF:], 1)
    mine = lax.dynamic_slice_in_dim(prefix, c, 2).astype(BF)
    limits = jnp.broadcast_to(jnp.pad(mine, (0, 14))[:, None], (16, 256))

    got0, got1, got2 = (shift(v, "zl", off) for v, off in zip(w, OFFS[1:]))
    tok_y = [shift(tok, "y", off) for off in OFFS[1:]]
    *tok_y, cot, got0, got1 = together(*tok_y, cot, got0, got1)
    up1, down1, up2, down2 = shift_z(cot, 1), shift_z(cot, -1), shift_z(cot, 2), shift_z(cot, -2)
    up1, down1, up2, down2, got2 = together(up1, down1, up2, down2, got2)
    placed = move(
        place_kernel, co, gate_weight, up_weight, down_weight, got0, got1, got2, out_shape=shape(768, 512)
    )
    weights = lax.all_gather(placed, ("x", "c"), axis=0, tiled=True)
    half = HALF // 2
    up3, down3, up4, down4 = together(
        shift_z(up2, 1), shift_z(down2, -1), shift_z(up2[:half], 2), shift_z(down2[half:], -2)
    )
    cot_in = [jnp.concatenate([cot, up1, down1, up2]), jnp.concatenate([down2, up3, down3, up4, down4])]
    tok_in = [jnp.concatenate([tok, *tok_y, limits])]
    up = down = tok_in[0]
    for _ in range(3):
        up, down = shift_z(up, 1), shift_z(down, -1)
        tok_in += [up, down]
    for _ in range(3):
        cot_in += [shift(cot_in[-2], "y", 1), shift(cot_in[-1], "y", -1)]
    tok_in += [shift_z(up[: ROWS // 2], 1), shift_z(down[ROWS // 2 : ROWS], -1)]

    mixed_terms, back_terms, terms = layer_call(co, tok_in, cot_in, weights)
    total = lax.psum_scatter(terms, ("x", "c"), scatter_dimension=0, tiled=True)

    up, down = shift_z(mixed_terms[7], 1), shift_z(mixed_terms[8], -1)
    half = ROWS // 2
    up = jnp.concatenate([add(mixed_terms[5][:half], up), mixed_terms[5][half:]])
    down = jnp.concatenate([mixed_terms[6][:half], add(mixed_terms[6][half:], down)])
    outer, inner = back_terms[7], back_terms[6]
    for k in (2, 1, 0):
        outer = add(back_terms[2 * k + 1], shift(outer, "y", -1))
        inner = add(back_terms[2 * k], shift(inner, "y", 1))
        if k > 0:
            up, down = shift_z(up, 1), shift_z(down, -1)
            up, down = add(mixed_terms[2 * k - 1], up), add(mixed_terms[2 * k], down)
    pieces = [v[n * HALF : (n + 1) * HALF] for v in (inner, outer) for n in range(4)]

    far, third_up, third_down = shift_z(pieces[7], 2), shift_z(pieces[5], 1), shift_z(pieces[6], -1)
    up, down = shift_z(up, 1), shift_z(down, -1)
    up, down, far, third_up, third_down = together(up, down, far, third_up, third_down)
    mixed = add(mixed_terms[0], up, down)
    up, down = add(pieces[3], third_up, far), add(pieces[4], third_down)
    near_up, near_down, up, down = shift_z(pieces[1], 1), shift_z(pieces[2], -1), shift_z(up, 2), shift_z(down, -2)
    mixed_y = [shift(mixed[o * HALF : (o + 1) * HALF], "y", OFFS[o]) for o in range(1, 4)]
    near_up, near_down, mixed_y[0], co = together(near_up, near_down, mixed_y[0], co)
    back = add(pieces[0], near_up, near_down, up, down)
    mixed = add(mixed[:HALF], *mixed_y)
    w = move(pack_back_kernel, co, total, out_shape=[shape(128, 768)] * 3)
    got = [shift(v, "zl", off) for v, off in zip(w, OFFS[1:])]
    mixed, back, got[0] = together(mixed, back, got[0])
    away = swap(jnp.concatenate([pick(mixed, 1 - c, 128, 1), pick(back, 1 - c, 128, 1)]))
    mixed = by_core(c, pick(mixed, c, 128, 1), away[:HALF], 0)
    input_grad = by_core(c, pick(back, c, 128, 1), away[HALF:], 0)
    gate_grad, up_grad, down_grad = move(
        place_back_kernel,
        co,
        total,
        *got,
        out_shape=[shape(128, 1024), shape(128, 1024), shape(1024, 128)],
    )
    return mixed, input_grad, gate_grad, up_grad, down_grad


def solution(mesh):
    fine = Mesh(mesh.devices.reshape(4, 4, 4, 2, 2), ("x", "zl", "y", "zh", "c"))
    rows, columns = ("x", "zl"), ("y", "zh", "c")
    return jax.shard_map(
        local,
        mesh=fine,
        in_specs=(
            P(rows, columns),
            P(rows, columns),
            P(rows),
            P(rows, columns),
            P(rows, columns),
            P(columns, rows),
        ),
        out_specs=(
            P(rows, columns),
            P(rows, columns),
            P(rows, columns),
            P(rows, columns),
            P(columns, rows),
        ),
        check_vma=False,
    )
```

```python
import math

import jax
import jax.numpy as jnp
from jax import lax
from jax.experimental import pallas as pl
from jax.experimental.pallas import tpu as pltpu
from jax.sharding import Mesh
from jax.sharding import PartitionSpec as P


D = 2048
TOK = 6144
BF = jnp.bfloat16
F32 = jnp.float32
HALF = 192
ROWS = 768
UNITS = 512
OFFS = (0, 1, -1, 2)
ZOFFS = (0, 1, -1, 2, -2, 3, -3, 4)
VMEM_LIMIT = 58 * 1024 * 1024
ANY = pl.BlockSpec(memory_space=pl.ANY)
VMEM = pl.BlockSpec(memory_space=pltpu.VMEM)
SMEM = pl.BlockSpec(memory_space=pltpu.SMEM)


def shift(value, axis, by):
    return lax.ppermute(value, axis, [(i, (i + by) % 4) for i in range(4)])


def shift_z(value, by):
    pairs = []
    for z in range(8):
        to = (z + by) % 8
        pairs.append(((z % 4) * 2 + z // 4, (to % 4) * 2 + to // 4))
    return lax.ppermute(value, ("zl", "zh"), pairs)


def together(*values):
    return lax.optimization_barrier(values)


def swap(value):
    return lax.ppermute(value, "c", [(0, 1), (1, 0)])


def run_copies(copies, sems, first=0):
    started = []
    for n, (src, dst) in enumerate(copies):
        copy = pltpu.make_async_copy(src, dst, sems.at[first + n])
        copy.start()
        started.append(copy)
    return started


def wait_all(started):
    for copy in started:
        copy.wait()


def spot(value, step):
    return pl.ds(pl.multiple_of(value * step, step), step)


def cost(flops, size):
    return pl.CostEstimate(flops=int(flops), bytes_accessed=int(size), transcendentals=0)


def shape(*dims):
    return jax.ShapeDtypeStruct(dims, BF)


def pack_kernel(co, gate, up, down, *outs):
    zl = co[1]
    for out, off in zip(outs, OFFS[1:]):
        to = lax.rem(zl + off + 4, 4)
        out[:, 0:256] = gate[:, spot(to, 256)]
        out[:, 256:512] = up[:, spot(to, 256)]
        for h in range(2):
            out[:, 512 + 128 * h : 640 + 128 * h] = down[spot(to * 2 + h, 128), :]


def place_kernel(co, gate, up, down, *rest):
    pieces, out = rest[:3], rest[3]
    zl = co[1]
    out[spot(zl, 128), 0:256] = gate[:, spot(zl, 256)]
    out[spot(zl, 128), 256:512] = up[:, spot(zl, 256)]
    out[512:768, spot(zl, 128)] = down[spot(zl, 256), :]
    for piece, off in zip(pieces, OFFS[1:]):
        at = lax.rem(zl - off + 4, 4)
        out[spot(at, 128), :] = piece[:, 0:512]
        for h in range(2):
            out[512 + 128 * h : 640 + 128 * h, spot(at, 128)] = piece[:, 512 + 128 * h : 640 + 128 * h]


def pack_back_kernel(co, total, *outs):
    zl = co[1]
    for out, off in zip(outs, OFFS[1:]):
        to = lax.rem(zl + off + 4, 4)
        out[:, 0:512] = total[spot(to, 128), :]
        for h in range(2):
            out[:, 512 + 128 * h : 640 + 128 * h] = total[512 + 128 * h : 640 + 128 * h, spot(to, 128)]


def place_back_kernel(co, total, *rest):
    pieces, (gate, up, down) = rest[:3], rest[3:6]
    zl = co[1]
    gate[:, spot(zl, 256)] = total[spot(zl, 128), 0:256]
    up[:, spot(zl, 256)] = total[spot(zl, 128), 256:512]
    down[spot(zl, 256), :] = total[512:768, spot(zl, 128)]
    for piece, off in zip(pieces, OFFS[1:]):
        at = lax.rem(zl - off + 4, 4)
        gate[:, spot(at, 256)] = piece[:, 0:256]
        up[:, spot(at, 256)] = piece[:, 256:512]
        for h in range(2):
            down[spot(at * 2 + h, 128), :] = piece[:, 512 + 128 * h : 640 + 128 * h]


def move(kernel, co, *args, out_shape):
    size = sum(a.size for a in args) * 2
    return pl.pallas_call(
        kernel,
        out_shape=out_shape,
        in_specs=[SMEM] + [VMEM] * len(args),
        out_specs=jax.tree.map(lambda _: VMEM, out_shape),
        cost_estimate=cost(0, size),
    )(co, *args)


def weight_copies(way, pieces, wide, down):
    gate_up, downs = [], []
    for x in range(4):
        for core in range(2):
            first = (x * 2 + core) * 768
            for part in range(2) if wide is not None else ():
                place = wide.at[pl.ds(x * 512, 512), pl.ds(512 * part + 256 * core, 256)]
                gate_up.append((pieces.at[pl.ds(first, 512), pl.ds(256 * part, 256)], place)[::way])
            if down is not None:
                place = down.at[pl.ds(256 * core, 256), pl.ds(x * 512, 512)]
                downs.append((pieces.at[pl.ds(first + 512, 256), :], place)[::way])
    return gate_up, downs


def whole_spot(y, z, whole):
    return whole.at[spot(lax.rem(z, 4), HALF), spot(y * 2 + z // 4, 256)]


def z_first_copies(co, way, pieces, whole):
    copies = []
    for n, off in enumerate(ZOFFS):
        at = lax.rem(co[5] - way * off + 8, 8)
        for o, y_off in enumerate(OFFS):
            piece = pieces[n] if n < 7 else pieces[7 + o // 2]
            src = piece.at[pl.ds((o if n < 7 else o % 2) * HALF, HALF), :]
            copies.append((src, whole_spot(lax.rem(co[2] - way * y_off + 4, 4), at, whole))[::way])
    return copies


def y_first_copies(co, way, pieces, whole):
    copies = []
    for k in range(4):
        for n, off in enumerate(ZOFFS):
            y = lax.rem(co[2] - way * k * (1 if n < 4 else -1) + 8, 4)
            src = pieces[2 * k + n // 4].at[pl.ds(n % 4 * HALF, HALF), :]
            copies.append((src, whole_spot(y, lax.rem(co[5] - way * off + 8, 8), whole))[::way])
    return copies


NN = (((1,), (0,)), ((), ()))
NT = (((1,), (1,)), ((), ()))


def dot(a, b, dims):
    return lax.dot_general(a, b, dims, preferred_element_type=F32)


def call(kernel, co, args, outs, scratch, sems, cost_estimate):
    return pl.pallas_call(
        kernel,
        out_shape=outs,
        in_specs=[SMEM] + [ANY] * len(args),
        out_specs=[ANY] * len(outs),
        scratch_shapes=[pltpu.VMEM(s, BF) for s in scratch] + [pltpu.SemaphoreType.DMA((sems,))],
        compiler_params=pltpu.CompilerParams(vmem_limit_bytes=VMEM_LIMIT),
        cost_estimate=cost_estimate,
    )(co, *args)


def layer_kernel(co, *refs):
    tok_in, cot_in, weights = refs[:9], refs[9:17], refs[17]
    mixed_out, back_out, terms_out = refs[18:27], refs[27:35], refs[35]
    tok, cot, wide, down, hid, grads, mixed, back, wide_grad, down_grad, limits, sems = refs[36:]
    zl, y, zh, c, z = co[1], co[2], co[3], co[4], co[5]
    scale = 1.0 / math.sqrt(TOK)
    gate_up, downs = weight_copies(1, weights, wide, down)
    limit_copies = []
    for n, off in enumerate(ZOFFS[:4]):
        at = lax.rem(z - off + 8, 4)
        limit_copies.append((tok_in[n].at[pl.ds(ROWS, 16), :], limits.at[spot(at, 16), :]))
    loads = gate_up + z_first_copies(co, 1, tok_in, tok) + limit_copies
    early = run_copies(loads, sems)
    late = run_copies(y_first_copies(co, 1, cot_in, cot) + downs, sems, len(early))
    used = len(early) + len(late)
    wait_all(early)
    split = 128 - 64 * c

    for m in range(2):
        part = pl.ds(m * 2 * HALF, 2 * HALF)
        pre = dot(tok[part, :], wide[...], NN)
        if m == 0:
            wait_all(late)
        grad_hidden = dot(cot[part, :], down[...], NT)
        for core in range(2):
            first = ((y * 2 + zh) * 2 + core) * 1024 + zl * 256
            unit = (first + lax.broadcasted_iota(jnp.int32, (HALF, 256), 1)).astype(F32)
            row = lax.broadcasted_iota(jnp.int32, (HALF, 256), 0)
            for block in range(2):
                limit = limits[pl.ds(16 * (2 * m + block), 16), :].astype(F32)
                keep = unit < jnp.where(row < split, limit[0:1], limit[1:2])
                near = slice(block * HALF, block * HALF + HALF)
                rows = pl.ds((2 * m + block) * HALF, HALF)
                g = pre[near, 256 * core : 256 * core + 256]
                u = pre[near, 512 + 256 * core : 768 + 256 * core]
                gh = grad_hidden[near, 256 * core : 256 * core + 256]
                sig = jax.nn.sigmoid(g)
                act = g * sig
                gate_part, up_part = pl.ds(256 * core, 256), pl.ds(512 + 256 * core, 256)
                hid[rows, gate_part] = jnp.where(keep, act * u, 0.0).astype(BF)
                grads[rows, gate_part] = jnp.where(
                    keep, gh * u * sig * (1.0 + g * (1.0 - sig)), 0.0
                ).astype(BF)
                grads[rows, up_part] = jnp.where(keep, gh * act, 0.0).astype(BF)

    @pl.loop(0, 2)
    def _(m):
        rows = spot(m, 384)
        mixed[rows, :] = dot(hid[rows, :], down[...], NN).astype(BF)

    kept = run_copies(z_first_copies(co, -1, mixed_out, mixed), sems, used)

    @pl.loop(0, 2)
    def _(m):
        rows = spot(m, 384)
        back[rows, :] = dot(grads[rows, :], wide[...], NT).astype(BF)

    kept += run_copies(y_first_copies(co, -1, back_out, back), sems, used + len(kept))

    @pl.loop(0, 2)
    def _(n):
        block = spot(n, 1024)
        wide_grad[block, :] = (dot(tok[:, block].T, grads[...], NN) * scale).astype(BF)

    gate_up, downs = weight_copies(-1, terms_out, wide_grad, down_grad)
    kept += run_copies(gate_up, sems, used + len(kept))
    down_grad[...] = (dot(hid[...].T, cot[...], NN) * scale).astype(BF)
    kept += run_copies(downs, sems, used + len(kept))
    wait_all(kept)


def layer_call(co, tok_in, cot_in, weights):
    outs = [shape(ROWS, 256) for _ in range(7)] + [shape(ROWS // 2, 256) for _ in range(2)]
    outs += [shape(4 * HALF, 256) for _ in range(8)] + [shape(8 * 768, 512)]
    out = call(
        layer_kernel,
        co,
        (*tok_in, *cot_in, weights),
        outs,
        [(ROWS, D), (ROWS, D), (D, 2 * UNITS), (UNITS, D), (ROWS, UNITS), (ROWS, 2 * UNITS), (ROWS, D)]
        + [(ROWS, D), (D, 2 * UNITS), (UNITS, D), (64, 256)],
        92 + 32 + 32 + 24,
        cost(18 * ROWS * D * UNITS, 30e6),
    )
    return out[:9], out[9:17], out[17]


def add(*terms):
    total = terms[0].astype(F32)
    for term in terms[1:]:
        total = total + term.astype(F32)
    return total.astype(BF)


def by_core(c, kept, got, axis):
    return jnp.where(c == 0, jnp.concatenate([kept, got], axis), jnp.concatenate([got, kept], axis))


def pick(value, at, size, axis):
    return lax.dynamic_slice_in_dim(value, at * size, size, axis)


def local(tokens, cotangent, prefix, gate_weight, up_weight, down_weight):
    x, zl, y, zh, c = (lax.axis_index(a) for a in ("x", "zl", "y", "zh", "c"))
    co = jnp.stack([x, zl, y, zh, c, zh * 4 + zl]).astype(jnp.int32)

    w = list(move(pack_kernel, co, gate_weight, up_weight, down_weight, out_shape=[shape(128, 768)] * 3))
    tokens, cotangent, *w = together(tokens, cotangent, *w)
    away = swap(jnp.concatenate([pick(tokens, 1 - c, HALF, 0), pick(cotangent, 1 - c, HALF, 0)]))
    tok = by_core(c, pick(tokens, c, HALF, 0), away[:HALF], 1)
    cot = by_core(c, pick(cotangent, c, HALF, 0), away[HALF:], 1)
    mine = lax.dynamic_slice_in_dim(prefix, c, 2).astype(BF)
    limits = jnp.broadcast_to(jnp.pad(mine, (0, 14))[:, None], (16, 256))

    got0, got1, got2 = (shift(v, "zl", off) for v, off in zip(w, OFFS[1:]))
    tok_y = [shift(tok, "y", off) for off in OFFS[1:]]
    *tok_y, cot, got0, got1 = together(*tok_y, cot, got0, got1)
    up1, down1, up2, down2 = shift_z(cot, 1), shift_z(cot, -1), shift_z(cot, 2), shift_z(cot, -2)
    up1, down1, up2, down2, got2 = together(up1, down1, up2, down2, got2)
    placed = move(
        place_kernel, co, gate_weight, up_weight, down_weight, got0, got1, got2, out_shape=shape(768, 512)
    )
    weights = lax.all_gather(placed, ("x", "c"), axis=0, tiled=True)
    up3, down3, up4 = together(shift_z(up2, 1), shift_z(down2, -1), shift_z(up2, 2))
    cot_in = [jnp.concatenate([cot, up1, down1, up2]), jnp.concatenate([down2, up3, down3, up4])]
    tok_in = [jnp.concatenate([tok, *tok_y, limits])]
    up = down = tok_in[0]
    for _ in range(3):
        up, down = shift_z(up, 1), shift_z(down, -1)
        tok_in += [up, down]
    for _ in range(3):
        cot_in += [shift(cot_in[-2], "y", 1), shift(cot_in[-1], "y", -1)]
    tok_in += [shift_z(up[: ROWS // 2], 1), shift_z(down[ROWS // 2 : ROWS], -1)]

    mixed_terms, back_terms, terms = layer_call(co, tok_in, cot_in, weights)
    total = lax.psum_scatter(terms, ("x", "c"), scatter_dimension=0, tiled=True)

    up, down = shift_z(mixed_terms[7], 1), shift_z(mixed_terms[8], -1)
    half = ROWS // 2
    up = jnp.concatenate([add(mixed_terms[5][:half], up), mixed_terms[5][half:]])
    down = jnp.concatenate([mixed_terms[6][:half], add(mixed_terms[6][half:], down)])
    outer, inner = back_terms[7], back_terms[6]
    for k in (2, 1, 0):
        outer = add(back_terms[2 * k + 1], shift(outer, "y", -1))
        inner = add(back_terms[2 * k], shift(inner, "y", 1))
        if k > 0:
            up, down = shift_z(up, 1), shift_z(down, -1)
            up, down = add(mixed_terms[2 * k - 1], up), add(mixed_terms[2 * k], down)
    pieces = [v[n * HALF : (n + 1) * HALF] for v in (inner, outer) for n in range(4)]

    far, third_up, third_down = shift_z(pieces[7], 2), shift_z(pieces[5], 1), shift_z(pieces[6], -1)
    up, down = shift_z(up, 1), shift_z(down, -1)
    up, down, far, third_up, third_down = together(up, down, far, third_up, third_down)
    mixed = add(mixed_terms[0], up, down)
    up, down = add(pieces[3], third_up, far), add(pieces[4], third_down)
    near_up, near_down, up, down = shift_z(pieces[1], 1), shift_z(pieces[2], -1), shift_z(up, 2), shift_z(down, -2)
    mixed_y = [shift(mixed[o * HALF : (o + 1) * HALF], "y", OFFS[o]) for o in range(1, 4)]
    near_up, near_down, mixed_y[0], co = together(near_up, near_down, mixed_y[0], co)
    back = add(pieces[0], near_up, near_down, up, down)
    mixed = add(mixed[:HALF], *mixed_y)
    w = move(pack_back_kernel, co, total, out_shape=[shape(128, 768)] * 3)
    got = [shift(v, "zl", off) for v, off in zip(w, OFFS[1:])]
    mixed, back, got[0] = together(mixed, back, got[0])
    away = swap(jnp.concatenate([pick(mixed, 1 - c, 128, 1), pick(back, 1 - c, 128, 1)]))
    mixed = by_core(c, pick(mixed, c, 128, 1), away[:HALF], 0)
    input_grad = by_core(c, pick(back, c, 128, 1), away[HALF:], 0)
    gate_grad, up_grad, down_grad = move(
        place_back_kernel,
        co,
        total,
        *got,
        out_shape=[shape(128, 1024), shape(128, 1024), shape(1024, 128)],
    )
    return mixed, input_grad, gate_grad, up_grad, down_grad


def solution(mesh):
    fine = Mesh(mesh.devices.reshape(4, 4, 4, 2, 2), ("x", "zl", "y", "zh", "c"))
    rows, columns = ("x", "zl"), ("y", "zh", "c")
    return jax.shard_map(
        local,
        mesh=fine,
        in_specs=(
            P(rows, columns),
            P(rows, columns),
            P(rows),
            P(rows, columns),
            P(rows, columns),
            P(columns, rows),
        ),
        out_specs=(
            P(rows, columns),
            P(rows, columns),
            P(rows, columns),
            P(rows, columns),
            P(columns, rows),
        ),
        check_vma=False,
    )
```
